256 devices in a mesh: leaf: 8 (over z), front: 32 (over x, y, core).
Axes of the slice: x: 4, y: 4, z: 8, core: 2. Of those that a mesh axis runs over, the one named last changes fastest.
Arguments:
- fronts_leaf: float32 [8, 2, 512, 1024], P('leaf', None, 'front'), may hold values from -1 to 1.5, as said below
- fronts_upper: float32 [7, 2, 512, 1024], P(None, None, 'front'), may hold values from -1 to 1.5, as said below
- block_map: int32 [14, 32], replicated, may hold values from 0 to 63, as said below
- parent_cov: float32 [512, 512], P('front'), may hold values from -1 to 1.5, as said below
Outputs:
- leaf_cov: float32 [8, 2, 512, 1024], P('leaf', None, 'front')
The draws below stay inside these ranges and needn't reach their ends.
Inputs may be any that keep to these rules, and one draw needn't show every extreme that they name: `block_map`: each row names 32 different blocks. `fronts_leaf`: every front is symmetric positive definite. `fronts_upper`: every front is symmetric positive definite. `parent_cov`: symmetric positive definite.
All inputs are finite; a program needn't handle non-finite values.
Results may differ from the reference program's by a relative error of at most 0.0001.
Values sent between devices are 32-bit elements; how exact they have to be, the bound alone decides.
A program may use at most 192 MiB of HBM per device.

```python
import jax
import jax.numpy as jnp
from jax import lax

H = 512
FRONT = 1024
BLOCK = 16
NB = 32
NBF = 64
LEAVES = 8
UPPER = 7
CHILDREN = 14
LEVELS = 4


def definite(key, matrix_count, matrix_order, spread):
    key_off = jax.random.fold_in(key, 11)
    key_diag = jax.random.fold_in(key, 23)
    half_width = spread / jnp.sqrt(jnp.float32(matrix_order))
    uniform_part = jax.random.uniform(key_off, (matrix_count, matrix_order, matrix_order), jnp.float32, -half_width, half_width)
    symmetric = (uniform_part + jnp.swapaxes(uniform_part, 1, 2)) * 0.7071
    diagonal = jax.random.uniform(key_diag, (matrix_count, matrix_order), jnp.float32, 0.6, 1.2)
    eye_mat = jnp.eye(matrix_order, dtype=jnp.float32)
    return symmetric * (1.0 - eye_mat) + diagonal[:, :, None] * eye_mat


def draw_fronts_leaf(key, part):
    return definite(jax.random.fold_in(key, 3), LEAVES, FRONT, 0.36).reshape(LEAVES, 2, H, FRONT)


def draw_fronts_upper(key, part):
    return definite(jax.random.fold_in(key, 5), UPPER, FRONT, 0.36).reshape(UPPER, 2, H, FRONT)


def draw_parent_cov(key, part):
    return definite(jax.random.fold_in(key, 7), 1, H, 0.36)[0]


def draw_block_map(key, part):
    row_keys = jax.random.split(jax.random.fold_in(key, 9), CHILDREN)
    chosen = jax.vmap(lambda one_key: jax.random.permutation(one_key, NBF)[:NB])(row_keys)
    return chosen.astype(jnp.int32)


def setup_inputs(seed: int = 0) -> dict:
    arg_keys = jax.random.split(jax.random.key(seed), 5)
    return {
        "fronts_leaf": draw_fronts_leaf(jax.random.fold_in(arg_keys[4], 71), 0),
        "fronts_upper": draw_fronts_upper(jax.random.fold_in(arg_keys[4], 71), 0),
        "block_map": draw_block_map(jax.random.fold_in(arg_keys[4], 71), 0),
        "parent_cov": draw_parent_cov(jax.random.fold_in(arg_keys[4], 71), 0),
    }


precise = lax.Precision.HIGHEST

def matmul(left_mat, right_mat):
    return jnp.dot(left_mat.astype(jnp.float32), right_mat.astype(jnp.float32), precision=precise, preferred_element_type=jnp.float32)

def factor(assembled):
    chol_top = jnp.linalg.cholesky(assembled[:H, :H])
    chol_low = lax.linalg.triangular_solve(chol_top, assembled[H:, :H], left_side=False, lower=True, transpose_a=True)
    schur_part = assembled[H:, H:] - matmul(chol_low, chol_low.T)
    return (chol_top, chol_low, schur_part)

def extend(parent, schur_part, blocks):
    tile_grid = schur_part.reshape(NB, BLOCK, NB, BLOCK).transpose(0, 2, 1, 3)
    front_grid = parent.reshape(NBF, BLOCK, NBF, BLOCK).transpose(0, 2, 1, 3)
    front_grid = front_grid.at[blocks[:, None], blocks[None, :]].add(tile_grid)
    return front_grid.transpose(0, 2, 1, 3).reshape(FRONT, FRONT)

def select(inverse, blocks):
    front_grid = inverse.reshape(NBF, BLOCK, NBF, BLOCK).transpose(0, 2, 1, 3)
    tile_grid = front_grid[blocks[:, None], blocks[None, :]]
    return tile_grid.transpose(0, 2, 1, 3).reshape(H, H)

def invert(chol_top, chol_low, lower_cov):
    eye_mat = jnp.eye(H, dtype=jnp.float32)
    inverse_low = lax.linalg.triangular_solve(chol_top, eye_mat, left_side=True, lower=True)
    cross_map = matmul(chol_low, inverse_low)
    cov_cross = -matmul(lower_cov, cross_map)
    cov_pivot = matmul(inverse_low.T, inverse_low) - matmul(cross_map.T, cov_cross)
    upper_half = jnp.concatenate([cov_pivot, cov_cross.T], 1)
    lower_half = jnp.concatenate([cov_cross, lower_cov], 1)
    return jnp.concatenate([upper_half, lower_half], 0)

def reference(fronts_leaf, fronts_upper, block_map, parent_cov):
    factors = [[factor(fronts_leaf[node_id].reshape(FRONT, FRONT)) for node_id in range(LEAVES)]]
    for height in range(1, LEVELS):
        map_base = 2 * LEAVES - 4 * LEAVES // 2 ** height
        upper_base = LEAVES - 2 * LEAVES // 2 ** height
        current = []
        for node_id in range(LEAVES // 2 ** height):
            parent = fronts_upper[upper_base + node_id].reshape(FRONT, FRONT)
            for sibling in range(2):
                child_id = 2 * node_id + sibling
                parent = extend(parent, factors[-1][child_id][2], block_map[map_base + child_id])
            current.append(factor(parent))
        factors.append(current)
    covariances = [parent_cov]
    inverses = []
    for height in range(LEVELS - 1, -1, -1):
        inverses = [invert(factors_now[0], factors_now[1], lower_cov) for factors_now, lower_cov in zip(factors[height], covariances)]
        if height > 0:
            map_base = 2 * LEAVES - 4 * LEAVES // 2 ** height
            covariances = [select(inverses[child_id // 2], block_map[map_base + child_id]) for child_id in range(2 * len(inverses))]
    return jnp.stack([inverse.reshape(2, H, FRONT) for inverse in inverses])
```

```python
import functools

import jax
import jax.numpy as jnp
from jax import lax
from jax.experimental import pallas as pl
from jax.experimental.pallas import tpu as pltpu
from jax.sharding import PartitionSpec as P

H = 512
FRONT = 1024
BLOCK = 16
NB = 32
NBF = 64
FD = 32
LEVELS = 4
MESH = pl.DeviceIdType.MESH
HI = lax.Precision.HIGHEST
F32 = jnp.float32


def dot(a, b):
    return jnp.dot(a, b, precision=HI, preferred_element_type=F32)


def dot_tn(a, b):
    return lax.dot_general(
        a, b, (((0,), (0,)), ((), ())), precision=HI, preferred_element_type=F32
    )


def inv128(groups):
    n = len(groups)
    sub = lax.broadcasted_iota(jnp.int32, (8, 128), 0)
    lane = lax.broadcasted_iota(jnp.int32, (8, 128), 1)
    mats = list(groups)

    def lanes_of(x, k):
        return jnp.broadcast_to(x[:, k : k + 1], (8, 128))

    def rows_of(x, k):
        return jnp.broadcast_to(x[k : k + 1, :], (8, 128))

    for g in range(n):
        cur = mats[g]
        cols = [lanes_of(cur, 8 * g + k) for k in range(8)]
        for j in range(8):
            e = sub == j
            ln = lane == 8 * g + j
            inv = 1.0 / rows_of(cols[j], j)
            mult = jnp.where(e, inv, -cols[j] * inv)
            row = jnp.where(ln, 1.0, rows_of(cur, j))
            cur = jnp.where(e | ln, 0.0, cur) + mult * row
            for k in range(j + 1, 8):
                cols[k] = jnp.where(e, 0.0, cols[k]) + mult * rows_of(cols[k], j)
        mats[g] = cur
        rows = [rows_of(cur, j) for j in range(8)]
        in_group = (lane >= 8 * g) & (lane < 8 * g + 8)
        for i in [(g + 1 + q) % n for q in range(n - 1)]:
            x = mats[i]
            t = [lanes_of(x, 8 * g + j) * rows[j] for j in range(8)]
            s = ((t[0] + t[1]) + (t[2] + t[3])) + ((t[4] + t[5]) + (t[6] + t[7]))
            mats[i] = jnp.where(in_group, 0.0, x) - s
    return mats


def invert_in_place(o_ref):
    def step(k, carry):
        ks = pl.multiple_of(k * 128, 128)
        g = [o_ref[pl.ds(ks + 8 * i, 8), pl.ds(ks, 128)] for i in range(16)]
        diag = jnp.concatenate(inv128(g), 0)
        rows = dot(diag, o_ref[pl.ds(ks, 128), :])
        col = o_ref[:, pl.ds(ks, 128)]
        row_id = lax.broadcasted_iota(jnp.int32, col.shape, 0)
        col = jnp.where((row_id >= ks) & (row_id < ks + 128), 0.0, col)
        o_ref[...] = o_ref[...] - dot(col, rows)
        o_ref[:, pl.ds(ks, 128)] = -dot(col, diag)
        o_ref[pl.ds(ks, 128), :] = rows
        o_ref[pl.ds(ks, 128), pl.ds(ks, 128)] = diag
        return carry

    lax.fori_loop(0, H // 128, step, 0)


def leaf_factor_kernel(top_ref, low_ref, ai_ref, s_ref, xt_ref, gt_ref):
    me = lax.axis_index("front")
    ai_ref[...] = top_ref[:, :H]
    invert_in_place(ai_ref)
    g = dot(low_ref[:, :H], ai_ref[...])
    s_ref[...] = low_ref[:, H:] - dot(g, top_ref[:, H:])
    rows = lax.broadcasted_iota(jnp.int32, (H, 2 * BLOCK), 0)
    cols = lax.broadcasted_iota(jnp.int32, (H, 2 * BLOCK), 1)
    za = (rows == me * BLOCK + cols).astype(F32)
    zb = (rows == (me - 1) * BLOCK + cols) & (cols >= BLOCK)
    za = jnp.where(cols < BLOCK, za, 0.0)
    gt = dot(ai_ref[...], za)
    gt_ref[...] = gt
    xt_ref[...] = zb.astype(F32) - dot_tn(top_ref[:, H:], gt)


def assemble(inv_ref, which, s_ref, zrow_ref, zt_ref, top_ref, low_ref, me):
    for p in range(NBF):
        a = inv_ref[which, p]
        ok = (a < NB).astype(F32)
        src = pl.multiple_of(jnp.minimum(a, NB - 1) * BLOCK, BLOCK)
        zrow_ref[pl.ds(p * BLOCK, BLOCK), :] = s_ref[pl.ds(src, BLOCK), :] * ok
    zt_ref[...] = zrow_ref[...].T
    for p in range(NB):
        a = inv_ref[which, p]
        ok = (a < NB).astype(F32)
        src = pl.multiple_of(jnp.minimum(a, NB - 1) * BLOCK, BLOCK)
        rows = pl.ds(p * BLOCK, BLOCK)
        top_ref[rows, :] = top_ref[rows, :] + zt_ref[pl.ds(src, BLOCK), :] * ok
    a = inv_ref[which, NB + me]
    ok = (a < NB).astype(F32)
    src = pl.multiple_of(jnp.minimum(a, NB - 1) * BLOCK, BLOCK)
    low_ref[...] = low_ref[...] + zt_ref[pl.ds(src, BLOCK), :] * ok


def upward(inv_ref, xt_child, zt_up, ai_ref, top_ref, gt_ref):
    for p in range(NBF):
        a = inv_ref[0, p]
        ok = (a < NB).astype(F32)
        src = pl.multiple_of(jnp.minimum(a, NB - 1) * BLOCK, BLOCK)
        zt_up[pl.ds(p * BLOCK, BLOCK), :] = xt_child[pl.ds(src, BLOCK), :] * ok
    gt = dot(ai_ref[...], zt_up[:H, :])
    gt_ref[...] = gt
    return zt_up[H:, :] - dot_tn(top_ref[:, H:], gt)


def mid_factor_kernel(
    inv_ref, init_ref, low_in_ref, own_ref, par_ref, xt_in_ref,
    ai_ref, top_ref, s_ref, xt_ref, gt_ref,
    zrow_ref, zt_ref, low_ref, zt_up,
):
    me = lax.axis_index("front")
    top_ref[...] = init_ref[...]
    low_ref[...] = low_in_ref[...]
    assemble(inv_ref, 0, own_ref, zrow_ref, zt_ref, top_ref, low_ref, me)
    assemble(inv_ref, 1, par_ref, zrow_ref, zt_ref, top_ref, low_ref, me)
    ai_ref[...] = top_ref[:, :H]
    invert_in_place(ai_ref)
    g = dot(low_ref[:, :H], ai_ref[...])
    s_ref[...] = low_ref[:, H:] - dot(g, top_ref[:, H:])
    xt_ref[...] = upward(inv_ref, xt_in_ref, zt_up, ai_ref, top_ref, gt_ref)


def top_kernel(
    inv_ref, map_ref, init_ref, own_ref, par_ref, xt_in_ref, cov_ref,
    ai0, ai1, ai2, top0, top1, top2, gt0, gt1, gt2,
    out_ref,
    ai_ref, top_ref, gt_ref, zrow_ref, zt_ref, low_ref, zt_up, rt_ref, yt_ref,
):
    me = lax.axis_index("front")
    top_ref[...] = init_ref[...]
    low_ref[...] = jnp.zeros_like(low_ref)
    assemble(inv_ref, 0, own_ref, zrow_ref, zt_ref, top_ref, low_ref, me)
    assemble(inv_ref, 1, par_ref, zrow_ref, zt_ref, top_ref, low_ref, me)
    ai_ref[...] = top_ref[:, :H]
    invert_in_place(ai_ref)
    xt = upward(inv_ref, xt_in_ref, zt_up, ai_ref, top_ref, gt_ref)
    yt_ref[...] = dot(cov_ref[...], xt)
    ais = (ai0, ai1, ai2, ai_ref)
    tops = (top0, top1, top2, top_ref)
    gts = (gt0, gt1, gt2, gt_ref)
    for height in range(LEVELS - 1, -1, -1):
        yt = yt_ref[...]
        rt_ref[:H, :] = gts[height][...] - dot(ais[height][...], dot(tops[height][:, H:], yt))
        rt_ref[H:, :] = yt
        if height > 0:
            for a in range(NB):
                src = pl.multiple_of(map_ref[height - 1, a] * BLOCK, BLOCK)
                yt_ref[pl.ds(a * BLOCK, BLOCK), :] = rt_ref[pl.ds(src, BLOCK), :]
    out_ref[...] = rt_ref[...].T.reshape(2, BLOCK, FRONT)


VM = pl.BlockSpec(memory_space=pltpu.VMEM)
SM = pl.BlockSpec(memory_space=pltpu.SMEM)
ANY = pl.BlockSpec(memory_space=pl.ANY)


def sds(*shape):
    return jax.ShapeDtypeStruct(shape, F32)


def factor_params():
    return pltpu.CompilerParams(vmem_limit_bytes=48 * 2**20)


def gather_kernel(x_ref, o_ref, send_sems, recv_sems, local_sem):
    leaf = lax.axis_index("leaf")
    me = lax.axis_index("front")
    barrier = pltpu.get_barrier_semaphore()

    def greet(k, c):
        pl.semaphore_signal(barrier, inc=1, device_id=(leaf, (me + k) % FD), device_id_type=MESH)
        return c

    lax.fori_loop(1, FD, greet, 0)
    local = pltpu.make_async_copy(x_ref, o_ref.at[pl.ds(me * BLOCK, BLOCK)], local_sem)
    local.start()
    pl.semaphore_wait(barrier, FD - 1)

    def copy(k, slot):
        return pltpu.make_async_remote_copy(
            src_ref=x_ref,
            dst_ref=o_ref.at[pl.ds(slot * BLOCK, BLOCK)],
            send_sem=send_sems.at[k],
            recv_sem=recv_sems.at[k],
            device_id=(leaf, (me + k) % FD),
            device_id_type=MESH,
        )

    def send(k, c):
        copy(k, me).start()
        return c

    def finish(k, c):
        copy(k, (me + FD - k) % FD).wait_recv()
        copy(k, me).wait_send()
        return c

    lax.fori_loop(1, FD, send, 0)
    local.wait()
    lax.fori_loop(1, FD, finish, 0)


def gather_rows(x, collective_id):
    width = x.shape[1]
    return pl.pallas_call(
        gather_kernel,
        out_shape=sds(FD * BLOCK, width),
        in_specs=[VM],
        out_specs=ANY,
        scratch_shapes=[
            pltpu.SemaphoreType.DMA((FD,)),
            pltpu.SemaphoreType.DMA((FD,)),
            pltpu.SemaphoreType.DMA,
        ],
        compiler_params=pltpu.CompilerParams(collective_id=collective_id, has_side_effects=True),
    )(x)


def exchange_kernel(
    apart, x_ref, own_ref, par_ref, held, send_sems, recv_sems, psend_sems, precv_sems, z_sems, local_sems
):
    leaf = lax.axis_index("leaf")
    me = lax.axis_index("front")
    partner = leaf + apart - 2 * apart * ((leaf // apart) % 2)
    barrier = pltpu.get_barrier_semaphore()

    def greet(k, c):
        pl.semaphore_signal(barrier, inc=1, device_id=(leaf, (me + k) % FD), device_id_type=MESH)
        return c

    pl.semaphore_signal(barrier, inc=1, device_id=(partner, me), device_id_type=MESH)
    lax.fori_loop(1, FD, greet, 0)
    mine = pl.ds(me * BLOCK, BLOCK)
    local = pltpu.make_async_copy(x_ref, own_ref.at[mine], local_sems.at[0])
    local.start()
    pl.semaphore_wait(barrier, FD)
    across = pltpu.make_async_remote_copy(
        src_ref=x_ref,
        dst_ref=held,
        send_sem=z_sems.at[0],
        recv_sem=z_sems.at[1],
        device_id=(partner, me),
        device_id_type=MESH,
    )
    across.start()

    def copy(src, dst, sends, recvs, k, slot):
        return pltpu.make_async_remote_copy(
            src_ref=src,
            dst_ref=dst.at[pl.ds(slot * BLOCK, BLOCK)],
            send_sem=sends.at[k],
            recv_sem=recvs.at[k],
            device_id=(leaf, (me + k) % FD),
            device_id_type=MESH,
        )

    def send_own(k, c):
        copy(x_ref, own_ref, send_sems, recv_sems, k, me).start()
        return c

    def send_par(k, c):
        copy(held, par_ref, psend_sems, precv_sems, k, me).start()
        return c

    def finish(k, c):
        back = (me + FD - k) % FD
        copy(x_ref, own_ref, send_sems, recv_sems, k, back).wait_recv()
        copy(held, par_ref, psend_sems, precv_sems, k, back).wait_recv()
        copy(x_ref, own_ref, send_sems, recv_sems, k, me).wait_send()
        copy(held, par_ref, psend_sems, precv_sems, k, me).wait_send()
        return c

    lax.fori_loop(1, FD, send_own, 0)
    across.wait()
    local_par = pltpu.make_async_copy(held, par_ref.at[mine], local_sems.at[1])
    local_par.start()
    lax.fori_loop(1, FD, send_par, 0)
    local.wait()
    local_par.wait()
    lax.fori_loop(1, FD, finish, 0)


def exchange(x, apart, collective_id):
    sems = pltpu.SemaphoreType.DMA
    return pl.pallas_call(
        functools.partial(exchange_kernel, apart),
        out_shape=[sds(H, H), sds(H, H)],
        in_specs=[VM],
        out_specs=[ANY, ANY],
        scratch_shapes=[
            pltpu.VMEM((BLOCK, H), F32),
            sems((FD,)), sems((FD,)), sems((FD,)), sems((FD,)), sems((2,)), sems((2,)),
        ],
        compiler_params=pltpu.CompilerParams(collective_id=collective_id, has_side_effects=True),
    )(x)


def body(fronts_leaf, fronts_upper, block_map, parent_cov):
    leaves = 8
    my_leaf = lax.axis_index("leaf")
    own_index, par_index, uppers = [], [], []
    for height in range(1, LEVELS):
        base = 2 * leaves - 4 * leaves // 2**height
        child = jnp.right_shift(my_leaf, height - 1)
        own_index.append(base + child)
        par_index.append(base + jnp.bitwise_xor(child, 1))
        node = leaves - 2 * leaves // 2**height + jnp.right_shift(my_leaf, height)
        uppers.append(lax.dynamic_index_in_dim(fronts_upper, node, 0, keepdims=False))
    own_maps = jnp.stack([lax.dynamic_index_in_dim(block_map, i, 0, keepdims=False) for i in own_index])
    par_maps = jnp.stack([lax.dynamic_index_in_dim(block_map, i, 0, keepdims=False) for i in par_index])
    maps = jnp.stack([own_maps, par_maps], 1)
    hit = maps[:, :, None, :] == jnp.arange(NBF, dtype=jnp.int32)[None, None, :, None]
    where_from = jnp.arange(NB, dtype=jnp.int32) - NB
    inverse_maps = NB + jnp.sum(jnp.where(hit, where_from, 0), -1, dtype=jnp.int32)

    top0 = gather_rows(fronts_leaf[0, 0], 0)
    inits = [lax.all_gather(u[0], "front", axis=0, tiled=True) for u in uppers]
    cov = lax.all_gather(parent_cov, "front", axis=0, tiled=True)

    ai0, s_own, xt, gt0 = pl.pallas_call(
        leaf_factor_kernel,
        out_shape=[sds(H, H), sds(BLOCK, H), sds(H, 2 * BLOCK), sds(H, 2 * BLOCK)],
        in_specs=[VM] * 2,
        out_specs=[VM] * 4,
        compiler_params=factor_params(),
    )(top0, fronts_leaf[0, 1])
    ais, tops, gts = [ai0], [top0], [gt0]
    for height in range(1, LEVELS - 1):
        own, par = exchange(s_own, 2 ** (height - 1), height)
        ai, top, s_own, xt, gt = pl.pallas_call(
            mid_factor_kernel,
            out_shape=[sds(H, H), sds(H, FRONT), sds(BLOCK, H), sds(H, 2 * BLOCK), sds(H, 2 * BLOCK)],
            in_specs=[SM] + [VM] * 5,
            out_specs=[VM] * 5,
            scratch_shapes=[
                pltpu.VMEM((FRONT, H), F32),
                pltpu.VMEM((H, FRONT), F32),
                pltpu.VMEM((BLOCK, FRONT), F32),
                pltpu.VMEM((FRONT, 2 * BLOCK), F32),
            ],
            compiler_params=factor_params(),
        )(inverse_maps[height - 1], inits[height - 1], uppers[height - 1][1], own, par, xt)
        ais.append(ai)
        tops.append(top)
        gts.append(gt)
    own, par = exchange(s_own, 2 ** (LEVELS - 2), LEVELS - 1)
    out = pl.pallas_call(
        top_kernel,
        out_shape=sds(2, BLOCK, FRONT),
        in_specs=[SM, SM] + [VM] * 14,
        out_specs=VM,
        scratch_shapes=[
            pltpu.VMEM((H, H), F32),
            pltpu.VMEM((H, FRONT), F32),
            pltpu.VMEM((H, 2 * BLOCK), F32),
            pltpu.VMEM((FRONT, H), F32),
            pltpu.VMEM((H, FRONT), F32),
            pltpu.VMEM((BLOCK, FRONT), F32),
            pltpu.VMEM((FRONT, 2 * BLOCK), F32),
            pltpu.VMEM((FRONT, 2 * BLOCK), F32),
            pltpu.VMEM((H, 2 * BLOCK), F32),
        ],
        compiler_params=factor_params(),
    )(inverse_maps[2], own_maps, inits[2], own, par, xt, cov, *ais, *tops, *gts)
    return out[None]


def solution(mesh):
    placed = (P("leaf", None, "front", None), P(None, None, "front", None), P(), P("front", None))
    return jax.shard_map(
        body, mesh=mesh, in_specs=placed, out_specs=P("leaf", None, "front", None), check_vma=False
    )
```

```python
import functools

import jax
import jax.numpy as jnp
from jax import lax
from jax.experimental import pallas as pl
from jax.experimental.pallas import tpu as pltpu
from jax.sharding import PartitionSpec as P

H = 512
FRONT = 1024
BLOCK = 16
NB = 32
NBF = 64
FD = 32
LEVELS = 4
MESH = pl.DeviceIdType.MESH
HI = lax.Precision.HIGHEST
F32 = jnp.float32


def dot(a, b):
    return jnp.dot(a, b, precision=HI, preferred_element_type=F32)


def dot_tn(a, b):
    return lax.dot_general(
        a, b, (((0,), (0,)), ((), ())), precision=HI, preferred_element_type=F32
    )


def inv128(groups):
    n = len(groups)
    sub = lax.broadcasted_iota(jnp.int32, (8, 128), 0)
    lane = lax.broadcasted_iota(jnp.int32, (8, 128), 1)
    mats = list(groups)

    def lanes_of(x, k):
        return jnp.broadcast_to(x[:, k : k + 1], (8, 128))

    def rows_of(x, k):
        return jnp.broadcast_to(x[k : k + 1, :], (8, 128))

    for g in range(n):
        cur = mats[g]
        cols = [lanes_of(cur, 8 * g + k) for k in range(8)]
        for j in range(8):
            e = sub == j
            ln = lane == 8 * g + j
            inv = 1.0 / rows_of(cols[j], j)
            mult = jnp.where(e, inv, -cols[j] * inv)
            row = jnp.where(ln, 1.0, rows_of(cur, j))
            cur = jnp.where(e | ln, 0.0, cur) + mult * row
            for k in range(j + 1, 8):
                cols[k] = jnp.where(e, 0.0, cols[k]) + mult * rows_of(cols[k], j)
        mats[g] = cur
        rows = [rows_of(cur, j) for j in range(8)]
        in_group = (lane >= 8 * g) & (lane < 8 * g + 8)
        for i in [(g + 1 + q) % n for q in range(n - 1)]:
            x = mats[i]
            t = [lanes_of(x, 8 * g + j) * rows[j] for j in range(8)]
            s = ((t[0] + t[1]) + (t[2] + t[3])) + ((t[4] + t[5]) + (t[6] + t[7]))
            mats[i] = jnp.where(in_group, 0.0, x) - s
    return mats


def invert_in_place(o_ref):
    def step(k, carry):
        ks = pl.multiple_of(k * 128, 128)
        g = [o_ref[pl.ds(ks + 8 * i, 8), pl.ds(ks, 128)] for i in range(16)]
        diag = jnp.concatenate(inv128(g), 0)
        rows = dot(diag, o_ref[pl.ds(ks, 128), :])
        col = o_ref[:, pl.ds(ks, 128)]
        row_id = lax.broadcasted_iota(jnp.int32, col.shape, 0)
        col = jnp.where((row_id >= ks) & (row_id < ks + 128), 0.0, col)
        o_ref[...] = o_ref[...] - dot(col, rows)
        o_ref[:, pl.ds(ks, 128)] = -dot(col, diag)
        o_ref[pl.ds(ks, 128), :] = rows
        o_ref[pl.ds(ks, 128), pl.ds(ks, 128)] = diag
        return carry

    lax.fori_loop(0, H // 128, step, 0)


def leaf_factor_kernel(a11_ref, a12_ref, low_ref, ai_ref, s_ref, xt_ref, gt_ref):
    me = lax.axis_index("front")
    ai_ref[...] = a11_ref[...]
    invert_in_place(ai_ref)
    g = dot(low_ref[:, :H], ai_ref[...])
    s_ref[...] = low_ref[:, H:] - dot(g, a12_ref[...])
    rows = lax.broadcasted_iota(jnp.int32, (H, 2 * BLOCK), 0)
    cols = lax.broadcasted_iota(jnp.int32, (H, 2 * BLOCK), 1)
    za = (rows == me * BLOCK + cols).astype(F32)
    zb = (rows == (me - 1) * BLOCK + cols) & (cols >= BLOCK)
    za = jnp.where(cols < BLOCK, za, 0.0)
    gt = dot(ai_ref[...], za)
    gt_ref[...] = gt
    xt_ref[...] = zb.astype(F32) - dot_tn(a12_ref[...], gt)


def assemble(inv_ref, which, s_ref, zrow_ref, zt_ref, ai_ref, a12_ref, low_ref, me):
    for p in range(NBF):
        a = inv_ref[which, p]
        ok = (a < NB).astype(F32)
        src = pl.multiple_of(jnp.minimum(a, NB - 1) * BLOCK, BLOCK)
        zrow_ref[pl.ds(p * BLOCK, BLOCK), :] = s_ref[pl.ds(src, BLOCK), :] * ok
    zt_ref[...] = zrow_ref[...].T
    for p in range(NB):
        a = inv_ref[which, p]
        ok = (a < NB).astype(F32)
        src = pl.multiple_of(jnp.minimum(a, NB - 1) * BLOCK, BLOCK)
        rows = pl.ds(p * BLOCK, BLOCK)
        block = zt_ref[pl.ds(src, BLOCK), :] * ok
        ai_ref[rows, :] = ai_ref[rows, :] + block[:, :H]
        a12_ref[rows, :] = a12_ref[rows, :] + block[:, H:]
    a = inv_ref[which, NB + me]
    ok = (a < NB).astype(F32)
    src = pl.multiple_of(jnp.minimum(a, NB - 1) * BLOCK, BLOCK)
    low_ref[...] = low_ref[...] + zt_ref[pl.ds(src, BLOCK), :] * ok


def upward(inv_ref, xt_child, zt_up, ai_ref, a12_ref, gt_ref):
    for p in range(NBF):
        a = inv_ref[0, p]
        ok = (a < NB).astype(F32)
        src = pl.multiple_of(jnp.minimum(a, NB - 1) * BLOCK, BLOCK)
        zt_up[pl.ds(p * BLOCK, BLOCK), :] = xt_child[pl.ds(src, BLOCK), :] * ok
    gt = dot(ai_ref[...], zt_up[:H, :])
    gt_ref[...] = gt
    return zt_up[H:, :] - dot_tn(a12_ref[...], gt)


def mid_factor_kernel(
    inv_ref, init_ref, low_in_ref, own_ref, par_ref, xt_in_ref,
    ai_ref, a12_ref, s_ref, xt_ref, gt_ref,
    zrow_ref, zt_ref, low_ref, zt_up,
):
    me = lax.axis_index("front")
    ai_ref[...] = init_ref[:, :H]
    a12_ref[...] = init_ref[:, H:]
    low_ref[...] = low_in_ref[...]
    assemble(inv_ref, 0, own_ref, zrow_ref, zt_ref, ai_ref, a12_ref, low_ref, me)
    assemble(inv_ref, 1, par_ref, zrow_ref, zt_ref, ai_ref, a12_ref, low_ref, me)
    invert_in_place(ai_ref)
    g = dot(low_ref[:, :H], ai_ref[...])
    s_ref[...] = low_ref[:, H:] - dot(g, a12_ref[...])
    xt_ref[...] = upward(inv_ref, xt_in_ref, zt_up, ai_ref, a12_ref, gt_ref)


def top_kernel(
    inv_ref, map_ref, init_ref, own_ref, par_ref, xt_in_ref, cov_ref,
    ai0, ai1, ai2, a12_0, a12_1, a12_2, gt0, gt1, gt2,
    out_ref,
    ai_ref, a12_ref, gt_ref, zrow_ref, zt_ref, low_ref, zt_up, rt_ref, yt_ref,
):
    me = lax.axis_index("front")
    ai_ref[...] = init_ref[:, :H]
    a12_ref[...] = init_ref[:, H:]
    low_ref[...] = jnp.zeros_like(low_ref)
    assemble(inv_ref, 0, own_ref, zrow_ref, zt_ref, ai_ref, a12_ref, low_ref, me)
    assemble(inv_ref, 1, par_ref, zrow_ref, zt_ref, ai_ref, a12_ref, low_ref, me)
    invert_in_place(ai_ref)
    xt = upward(inv_ref, xt_in_ref, zt_up, ai_ref, a12_ref, gt_ref)
    yt_ref[...] = dot(cov_ref[...], xt)
    ais = (ai0, ai1, ai2, ai_ref)
    offs = (a12_0, a12_1, a12_2, a12_ref)
    gts = (gt0, gt1, gt2, gt_ref)
    for height in range(LEVELS - 1, -1, -1):
        yt = yt_ref[...]
        rt_ref[:H, :] = gts[height][...] - dot(ais[height][...], dot(offs[height][...], yt))
        rt_ref[H:, :] = yt
        if height > 0:
            for a in range(NB):
                src = pl.multiple_of(map_ref[height - 1, a] * BLOCK, BLOCK)
                yt_ref[pl.ds(a * BLOCK, BLOCK), :] = rt_ref[pl.ds(src, BLOCK), :]
    out_ref[...] = rt_ref[...].T.reshape(2, BLOCK, FRONT)


VM = pl.BlockSpec(memory_space=pltpu.VMEM)
SM = pl.BlockSpec(memory_space=pltpu.SMEM)
ANY = pl.BlockSpec(memory_space=pl.ANY)


def sds(*shape):
    return jax.ShapeDtypeStruct(shape, F32)


def factor_params():
    return pltpu.CompilerParams(vmem_limit_bytes=48 * 2**20)


def exchange_kernel(apart, x_ref, *refs):
    if apart:
        own, par, held, sends, recvs, z_sems, local_sems = refs
    else:
        held, own, par, sends, recvs, z_sems, local_sems = refs
    leaf = lax.axis_index("leaf")
    me = lax.axis_index("front")
    xi, yi, core = me // 8, (me // 2) % 4, me % 2
    sibling = (leaf, me + 1 - 2 * core)
    along_x = [None] + [(leaf, ((xi + k) % 4) * 8 + yi * 2 + core) for k in range(1, 4)]
    along_y = [None] + [(leaf, xi * 8 + ((yi + k) % 4) * 2 + core) for k in range(1, 4)]
    partners = along_x[1:] + along_y[1:] + [sibling]
    if apart:
        across_to = (leaf + apart - 2 * apart * ((leaf // apart) % 2), me)
        partners = partners + [across_to]
    barrier = pltpu.get_barrier_semaphore()
    for device in partners:
        pl.semaphore_signal(barrier, inc=1, device_id=device, device_id_type=MESH)
    own_local = pltpu.make_async_copy(x_ref, own.at[xi, yi, core], local_sems.at[0])
    own_local.start()
    pl.semaphore_wait(barrier, len(partners))

    def copy(stage, k, src, dst, device):
        return pltpu.make_async_remote_copy(
            src_ref=src,
            dst_ref=dst,
            send_sem=sends.at[stage, k],
            recv_sem=recvs.at[stage, k],
            device_id=device,
            device_id_type=MESH,
        )

    if apart:
        across = pltpu.make_async_remote_copy(
            src_ref=x_ref, dst_ref=held, send_sem=z_sems.at[0], recv_sem=z_sems.at[1],
            device_id=across_to, device_id_type=MESH,
        )
        across.start()
    order = (2, 1, 3)
    started = []

    def start(stage, k, src, dst, device):
        c = copy(stage, k, src, dst, device)
        c.start()
        started.append(c)

    for k in order:
        start(0, k, x_ref, own.at[xi, yi, core], along_x[k])
    if apart:
        across.wait_recv()
    par_local = pltpu.make_async_copy(held, par.at[xi, yi, core], local_sems.at[1])
    par_local.start()
    for k in order:
        start(1, k, held, par.at[xi, yi, core], along_y[k])
    own_local.wait()
    for k in (1, 3, 2):
        copy(0, k, x_ref, own.at[(xi + 4 - k) % 4, yi, core], along_x[k]).wait_recv()
    column = own.at[:, yi, core]
    for k in order:
        start(2, k, column, column, along_y[k])
    start(4, 0, column, column, sibling)
    par_local.wait()
    for k in (1, 3, 2):
        copy(1, k, held, par.at[xi, (yi + 4 - k) % 4, core], along_y[k]).wait_recv()
    column = par.at[xi, :, core]
    for k in order:
        start(3, k, column, column, along_x[k])
    start(5, 0, column, column, sibling)
    for k in (1, 3, 2):
        column = own.at[:, (yi + 4 - k) % 4, core]
        copy(2, k, column, column, along_y[k]).wait_recv()
        start(4, k, column, column, sibling)
    for k in (1, 3, 2):
        column = par.at[(xi + 4 - k) % 4, :, core]
        copy(3, k, column, column, along_x[k]).wait_recv()
        start(5, k, column, column, sibling)
    for k in (0, 1, 3, 2):
        column = own.at[:, (yi + 4 - k) % 4, 1 - core]
        copy(4, k, column, column, sibling).wait_recv()
        column = par.at[(xi + 4 - k) % 4, :, 1 - core]
        copy(5, k, column, column, sibling).wait_recv()
    for c in started:
        c.wait_send()
    if apart:
        across.wait_send()


def exchange(arrays, apart, collective_id):
    sems = pltpu.SemaphoreType.DMA
    shape = sds(4, 4, 2, BLOCK, H)
    own, par = pl.pallas_call(
        functools.partial(exchange_kernel, apart),
        out_shape=[shape, shape],
        in_specs=[VM] * len(arrays),
        out_specs=[ANY, ANY],
        scratch_shapes=([pltpu.VMEM((BLOCK, H), F32)] if apart else [])
        + [sems((6, 4)), sems((6, 4)), sems((2,)), sems((2,))],
        compiler_params=pltpu.CompilerParams(collective_id=collective_id, has_side_effects=True),
    )(*arrays)
    return own.reshape(H, H), par.reshape(H, H)


def body(fronts_leaf, fronts_upper, block_map, parent_cov):
    leaves = 8
    my_leaf = lax.axis_index("leaf")
    own_index, par_index, uppers = [], [], []
    for height in range(1, LEVELS):
        base = 2 * leaves - 4 * leaves // 2**height
        child = jnp.right_shift(my_leaf, height - 1)
        own_index.append(base + child)
        par_index.append(base + jnp.bitwise_xor(child, 1))
        node = leaves - 2 * leaves // 2**height + jnp.right_shift(my_leaf, height)
        uppers.append(lax.dynamic_index_in_dim(fronts_upper, node, 0, keepdims=False))
    own_maps = jnp.stack([lax.dynamic_index_in_dim(block_map, i, 0, keepdims=False) for i in own_index])
    par_maps = jnp.stack([lax.dynamic_index_in_dim(block_map, i, 0, keepdims=False) for i in par_index])
    maps = jnp.stack([own_maps, par_maps], 1)
    hit = maps[:, :, None, :] == jnp.arange(NBF, dtype=jnp.int32)[None, None, :, None]
    where_from = jnp.arange(NB, dtype=jnp.int32) - NB
    inverse_maps = NB + jnp.sum(jnp.where(hit, where_from, 0), -1, dtype=jnp.int32)

    first = fronts_leaf[0, 0]
    a11, a12 = exchange([first[:, :H], first[:, H:]], 0, 0)
    inits = [lax.all_gather(u[0], "front", axis=0, tiled=True) for u in uppers]
    cov = lax.all_gather(parent_cov, "front", axis=0, tiled=True)

    ai0, s_own, xt, gt0 = pl.pallas_call(
        leaf_factor_kernel,
        out_shape=[sds(H, H), sds(BLOCK, H), sds(H, 2 * BLOCK), sds(H, 2 * BLOCK)],
        in_specs=[VM] * 3,
        out_specs=[VM] * 4,
        compiler_params=factor_params(),
    )(a11, a12, fronts_leaf[0, 1])
    ais, offs, gts = [ai0], [a12], [gt0]
    for height in range(1, LEVELS - 1):
        own, par = exchange([s_own], 2 ** (height - 1), height)
        ai, off, s_own, xt, gt = pl.pallas_call(
            mid_factor_kernel,
            out_shape=[sds(H, H), sds(H, H), sds(BLOCK, H), sds(H, 2 * BLOCK), sds(H, 2 * BLOCK)],
            in_specs=[SM] + [VM] * 5,
            out_specs=[VM] * 5,
            scratch_shapes=[
                pltpu.VMEM((FRONT, H), F32),
                pltpu.VMEM((H, FRONT), F32),
                pltpu.VMEM((BLOCK, FRONT), F32),
                pltpu.VMEM((FRONT, 2 * BLOCK), F32),
            ],
            compiler_params=factor_params(),
        )(inverse_maps[height - 1], inits[height - 1], uppers[height - 1][1], own, par, xt)
        ais.append(ai)
        offs.append(off)
        gts.append(gt)
    own, par = exchange([s_own], 2 ** (LEVELS - 2), LEVELS - 1)
    out = pl.pallas_call(
        top_kernel,
        out_shape=sds(2, BLOCK, FRONT),
        in_specs=[SM, SM] + [VM] * 14,
        out_specs=VM,
        scratch_shapes=[
            pltpu.VMEM((H, H), F32),
            pltpu.VMEM((H, H), F32),
            pltpu.VMEM((H, 2 * BLOCK), F32),
            pltpu.VMEM((FRONT, H), F32),
            pltpu.VMEM((H, FRONT), F32),
            pltpu.VMEM((BLOCK, FRONT), F32),
            pltpu.VMEM((FRONT, 2 * BLOCK), F32),
            pltpu.VMEM((FRONT, 2 * BLOCK), F32),
            pltpu.VMEM((H, 2 * BLOCK), F32),
        ],
        compiler_params=factor_params(),
    )(inverse_maps[2], own_maps, inits[2], own, par, xt, cov, *ais, *offs, *gts)
    return out[None]


def solution(mesh):
    placed = (P("leaf", None, "front", None), P(None, None, "front", None), P(), P("front", None))
    return jax.shard_map(
        body, mesh=mesh, in_specs=placed, out_specs=P("leaf", None, "front", None), check_vma=False
    )
```

```python
import jax
import jax.numpy as jnp
from jax import lax
from jax.experimental import pallas as pl
from jax.experimental.pallas import tpu as pltpu
from jax.sharding import PartitionSpec as P

H = 512
FRONT = 1024
BLOCK = 16
NB = 32
NBF = 64
FD = 32
LEVELS = 4
MESH = pl.DeviceIdType.MESH
HI = lax.Precision.HIGHEST
F32 = jnp.float32


def dot(a, b):
    return jnp.dot(a, b, precision=HI, preferred_element_type=F32)


def dot_tn(a, b):
    return lax.dot_general(
        a, b, (((0,), (0,)), ((), ())), precision=HI, preferred_element_type=F32
    )


def inv128(groups):
    n = len(groups)
    sub = lax.broadcasted_iota(jnp.int32, (8, 128), 0)
    lane = lax.broadcasted_iota(jnp.int32, (8, 128), 1)
    mats = list(groups)

    def lanes_of(x, k):
        return jnp.broadcast_to(x[:, k : k + 1], (8, 128))

    def rows_of(x, k):
        return jnp.broadcast_to(x[k : k + 1, :], (8, 128))

    for g in range(n):
        cur = mats[g]
        cols = [lanes_of(cur, 8 * g + k) for k in range(8)]
        for j in range(8):
            e = sub == j
            ln = lane == 8 * g + j
            inv = 1.0 / rows_of(cols[j], j)
            mult = jnp.where(e, inv, -cols[j] * inv)
            row = jnp.where(ln, 1.0, rows_of(cur, j))
            cur = jnp.where(e | ln, 0.0, cur) + mult * row
            for k in range(j + 1, 8):
                cols[k] = jnp.where(e, 0.0, cols[k]) + mult * rows_of(cols[k], j)
        mats[g] = cur
        rows = [rows_of(cur, j) for j in range(8)]
        in_group = (lane >= 8 * g) & (lane < 8 * g + 8)
        for i in [(g + 1 + q) % n for q in range(n - 1)]:
            x = mats[i]
            t = [lanes_of(x, 8 * g + j) * rows[j] for j in range(8)]
            s = ((t[0] + t[1]) + (t[2] + t[3])) + ((t[4] + t[5]) + (t[6] + t[7]))
            mats[i] = jnp.where(in_group, 0.0, x) - s
    return mats


def invert_in_place(o_ref, pumps):
    def step(k, carry):
        for at, pump in enumerate(pumps):
            if pump is not None:
                pl.when(k == at)(pump)
        ks = pl.multiple_of(k * 128, 128)
        g = [o_ref[pl.ds(ks + 8 * i, 8), pl.ds(ks, 128)] for i in range(16)]
        diag = jnp.concatenate(inv128(g), 0)
        rows = dot(diag, o_ref[pl.ds(ks, 128), :])
        col = o_ref[:, pl.ds(ks, 128)]
        row_id = lax.broadcasted_iota(jnp.int32, col.shape, 0)
        col = jnp.where((row_id >= ks) & (row_id < ks + 128), 0.0, col)
        o_ref[...] = o_ref[...] - dot(col, rows)
        o_ref[:, pl.ds(ks, 128)] = -dot(col, diag)
        o_ref[pl.ds(ks, 128), :] = rows
        o_ref[pl.ds(ks, 128), pl.ds(ks, 128)] = diag
        return carry

    lax.fori_loop(0, H // 128, step, 0)


class Flow:
    def __init__(self, buf, x_first, number, place, sends, recvs):
        self.buf, self.x_first, self.number = buf, x_first, number
        self.place, self.sends, self.recvs = place, sends, recvs
        self.started = []

    def slot(self, back=0):
        _, xi, yi, core = self.place
        if self.x_first:
            return self.buf.at[(xi + 4 - back) % 4, yi, core]
        return self.buf.at[xi, (yi + 4 - back) % 4, core]

    def line(self, back=0, other=False):
        _, xi, yi, core = self.place
        core = 1 - core if other else core
        if self.x_first:
            return self.buf.at[:, (yi + 4 - back) % 4, core]
        return self.buf.at[(xi + 4 - back) % 4, :, core]

    def device(self, along_x, k):
        leaf, xi, yi, core = self.place
        if along_x:
            return (leaf, ((xi + k) % 4) * 8 + yi * 2 + core)
        return (leaf, xi * 8 + ((yi + k) % 4) * 2 + core)

    def sibling(self):
        leaf, xi, yi, core = self.place
        return (leaf, xi * 8 + yi * 2 + 1 - core)

    def copy(self, sem, ref, device):
        return pltpu.make_async_remote_copy(
            src_ref=ref, dst_ref=ref,
            send_sem=self.sends.at[self.number, sem], recv_sem=self.recvs.at[self.number, sem],
            device_id=device, device_id_type=MESH,
        )

    def start(self, *args):
        c = self.copy(*args)
        c.start()

    def put(self, rows):
        _, xi, yi, core = self.place
        self.buf[xi, yi, core] = rows

    def first(self):
        for k in (2, 1, 3):
            self.start(k - 1, self.slot(), self.device(self.x_first, k))

    def second(self):
        for k in (1, 3, 2):
            self.copy(k - 1, self.slot(k), self.device(self.x_first, k)).wait_recv()
        for k in (2, 1, 3):
            self.start(2 + k, self.line(), self.device(not self.x_first, k))
        self.start(6, self.line(), self.sibling())

    def third(self):
        for k in (1, 3, 2):
            self.copy(2 + k, self.line(k), self.device(not self.x_first, k)).wait_recv()
            self.start(6 + k, self.line(k), self.sibling())

    def finish(self):
        for k in (0, 1, 3, 2):
            self.copy(6 + k, self.line(k, True), self.sibling()).wait_recv()
        for k in (1, 2, 3):
            self.copy(k - 1, self.slot(), self.device(self.x_first, k)).wait_send()
            self.copy(2 + k, self.line(), self.device(not self.x_first, k)).wait_send()
        for k in range(4):
            self.copy(6 + k, self.line(k), self.sibling()).wait_send()


def whole(ref):
    return ref[...].reshape(H, H)


def assemble(inv_ref, link, which, s_ref, blocks_ref, zrow_ref, zt_ref, ai_ref, a12_ref, low_ref, me):
    blocks_ref[:NB] = s_ref[...].reshape(NB, BLOCK, H)
    for p in range(NBF):
        zrow_ref[p] = blocks_ref[inv_ref[link, which, p]]
    zt_ref[:NB] = zrow_ref[...].reshape(FRONT, H).T.reshape(NB, BLOCK, FRONT)
    for p in range(NB):
        rows = pl.ds(p * BLOCK, BLOCK)
        block = zt_ref[inv_ref[link, which, p]]
        ai_ref[rows, :] = ai_ref[rows, :] + block[:, :H]
        a12_ref[rows, :] = a12_ref[rows, :] + block[:, H:]
    low_ref[...] = low_ref[...] + zt_ref[inv_ref[link, which, NB + me]]


def main_kernel(inv_ref, map_ref, leaf_ref, upper_ref, cov_ref, out_ref, *scratch):
    scratch = list(scratch)

    def take(n):
        got = scratch[:n]
        del scratch[:n]
        return got

    g11, g12, s_own, s_par = take(4), take(4), take(3), take(3)
    (gcov,) = take(1)
    ai, a12, gts, xts = take(4), take(4), take(4), take(4)
    blocks, zrow, zt, low, zt_up, rt, yt_ref, sends, recvs, z_sems = scratch
    blocks[NB] = jnp.zeros((BLOCK, H), F32)
    zt[NB] = jnp.zeros((BLOCK, FRONT), F32)
    for xt_ref in xts:
        xt_ref[NB] = jnp.zeros((BLOCK, 2 * BLOCK), F32)

    leaf = lax.axis_index("leaf")
    me = lax.axis_index("front")
    xi, yi, core = me // 8, (me // 2) % 4, me % 2
    place = (leaf, xi, yi, core)
    across_to = [(leaf + d - 2 * d * ((leaf // d) % 2), me) for d in (1, 2, 4)]
    partners = [(leaf, ((xi + k) % 4) * 8 + yi * 2 + core) for k in (1, 2, 3)]
    partners += [(leaf, xi * 8 + ((yi + k) % 4) * 2 + core) for k in (1, 2, 3)]
    partners += [(leaf, me + 1 - 2 * core)] + across_to
    barrier = pltpu.get_barrier_semaphore()
    for device in partners:
        pl.semaphore_signal(barrier, inc=1, device_id=device, device_id_type=MESH)

    numbers = iter(range(15))
    front_flows = [
        (Flow(g11[h], True, next(numbers), place, sends, recvs), Flow(g12[h], False, next(numbers), place, sends, recvs))
        for h in range(LEVELS)
    ]
    cov_flow = Flow(gcov, True, next(numbers), place, sends, recvs)
    schur_flows = [
        (Flow(s_own[h], True, next(numbers), place, sends, recvs), Flow(s_par[h], False, next(numbers), place, sends, recvs))
        for h in range(LEVELS - 1)
    ]
    nodes = [None, leaf // 2, 4 + leaf // 4, 6]

    def open_flows(height):
        if height == 0:
            front_flows[0][0].put(leaf_ref[0, 0, :, :H])
            front_flows[0][1].put(leaf_ref[0, 0, :, H:])
        else:
            front_flows[height][0].put(upper_ref[nodes[height], 0, :, :H])
            front_flows[height][1].put(upper_ref[nodes[height], 0, :, H:])
        for flow in front_flows[height]:
            flow.first()

    def pumps(flows, opening):
        def second():
            for flow in flows:
                flow.second()

        def third():
            for flow in flows:
                flow.third()

        def finish():
            for flow in flows:
                flow.finish()

        return (opening, second, third, finish)

    front_flows[0][0].put(leaf_ref[0, 0, :, :H])
    front_flows[0][1].put(leaf_ref[0, 0, :, H:])
    pl.semaphore_wait(barrier, len(partners))
    for flow in front_flows[0]:
        flow.first()
    for flow in front_flows[0]:
        flow.second()
    for flow in front_flows[0]:
        flow.third()
    front_flows[0][0].finish()
    ai[0][...] = whole(g11[0])
    front_flows[0][1].finish()
    a12[0][...] = whole(g12[0])
    low[...] = leaf_ref[0, 1]

    for height in range(LEVELS):
        last = height == LEVELS - 1
        if height > 0:
            ai[height][...] = whole(g11[height])
            a12[height][...] = whole(g12[height])
            low[...] = upper_ref[nodes[height], 1]
            for which, (flow, s_ref) in enumerate(zip(schur_flows[height - 1], (s_own[height - 1], s_par[height - 1]))):
                flow.finish()
                assemble(inv_ref, height - 1, which, s_ref, blocks, zrow, zt, ai[height], a12[height], low, me)
        if last:
            def opening():
                cov_flow.put(cov_ref[...])
                cov_flow.first()

            invert_in_place(ai[height], pumps([cov_flow], opening))
        else:
            def opening(above=height + 1):
                open_flows(above)

            invert_in_place(ai[height], pumps(front_flows[height + 1], opening))
            own_flow, par_flow = schur_flows[height]
            g = dot(low[:, :H], ai[height][...])
            own_flow.put(low[:, H:] - dot(g, a12[height][...]))
            across = pltpu.make_async_remote_copy(
                src_ref=s_own[height].at[xi, yi, core], dst_ref=s_par[height].at[xi, yi, core],
                send_sem=z_sems.at[height, 0], recv_sem=z_sems.at[height, 1],
                device_id=across_to[height], device_id_type=MESH,
            )
            across.start()
            own_flow.first()
        if height == 0:
            rows = lax.broadcasted_iota(jnp.int32, (H, 2 * BLOCK), 0)
            cols = lax.broadcasted_iota(jnp.int32, (H, 2 * BLOCK), 1)
            za = ((rows == me * BLOCK + cols) & (cols < BLOCK)).astype(F32)
            zb = ((rows == (me - 1) * BLOCK + cols) & (cols >= BLOCK)).astype(F32)
        else:
            for p in range(NBF):
                zt_up[pl.ds(p * BLOCK, BLOCK), :] = xts[height - 1][inv_ref[height - 1, 0, p]]
            za, zb = zt_up[:H, :], zt_up[H:, :]
        gt = dot(ai[height][...], za)
        gts[height][...] = gt
        xt = zb - dot_tn(a12[height][...], gt)
        xts[height][:NB] = xt.reshape(NB, BLOCK, 2 * BLOCK)
        if not last:
            across.wait_recv()
            par_flow.first()
            own_flow.second()
            par_flow.second()
            own_flow.third()
            par_flow.third()
            across.wait_send()

    yt_ref[...] = dot(whole(gcov), xt)
    for height in range(LEVELS - 1, -1, -1):
        yt = yt_ref[...]
        top = gts[height][...] - dot(ai[height][...], dot(a12[height][...], yt))
        rt[:NB] = top.reshape(NB, BLOCK, 2 * BLOCK)
        rt[NB:] = yt.reshape(NB, BLOCK, 2 * BLOCK)
        if height > 0:
            for a in range(NB):
                yt_ref[pl.ds(a * BLOCK, BLOCK), :] = rt[map_ref[height - 1, a]]
    out_ref[...] = rt[...].reshape(FRONT, 2 * BLOCK).T.reshape(1, 2, BLOCK, FRONT)


def body(fronts_leaf, fronts_upper, block_map, parent_cov):
    leaves = 8
    my_leaf = lax.axis_index("leaf")
    own_index = []
    for height in range(1, LEVELS):
        child = jnp.right_shift(my_leaf, height - 1)
        own_index.append(2 * leaves - 4 * leaves // 2**height + child)
    index = jnp.stack([jnp.stack([i, jnp.bitwise_xor(i, 1)]) for i in own_index])
    maps = block_map[index]
    hit = maps[:, :, None, :] == jnp.arange(NBF, dtype=jnp.int32)[None, None, :, None]
    where_from = jnp.arange(NB, dtype=jnp.int32) - NB
    inverse_maps = NB + jnp.sum(jnp.where(hit, where_from, 0), -1, dtype=jnp.int32)
    vm = pl.BlockSpec(memory_space=pltpu.VMEM)
    sm = pl.BlockSpec(memory_space=pltpu.SMEM)
    plane = pltpu.VMEM((4, 4, 2, BLOCK, H), F32)
    square = pltpu.VMEM((H, H), F32)
    thin = pltpu.VMEM((H, 2 * BLOCK), F32)
    parts = pltpu.VMEM((NB + 1, BLOCK, 2 * BLOCK), F32)
    sems = pltpu.SemaphoreType.DMA
    return pl.pallas_call(
        main_kernel,
        out_shape=jax.ShapeDtypeStruct((1, 2, BLOCK, FRONT), F32),
        in_specs=[sm, sm, vm, vm, vm],
        out_specs=vm,
        scratch_shapes=[plane] * 15 + [square] * 8 + [thin] * 4 + [parts] * 4
        + [
            pltpu.VMEM((NB + 1, BLOCK, H), F32),
            pltpu.VMEM((NBF, BLOCK, H), F32),
            pltpu.VMEM((NB + 1, BLOCK, FRONT), F32),
            pltpu.VMEM((BLOCK, FRONT), F32),
            pltpu.VMEM((FRONT, 2 * BLOCK), F32),
            pltpu.VMEM((NBF, BLOCK, 2 * BLOCK), F32),
            pltpu.VMEM((H, 2 * BLOCK), F32),
            sems((15, 10)), sems((15, 10)), sems((3, 2)),
        ],
        compiler_params=pltpu.CompilerParams(
            collective_id=0, has_side_effects=True, vmem_limit_bytes=56 * 2**20
        ),
    )(inverse_maps, maps[:, 0], fronts_leaf, fronts_upper, parent_cov)


def solution(mesh):
    placed = (P("leaf", None, "front", None), P(None, None, "front", None), P(), P("front", None))
    return jax.shard_map(
        body, mesh=mesh, in_specs=placed, out_specs=P("leaf", None, "front", None), check_vma=False
    )
```

```python
import jax
import jax.numpy as jnp
from jax import lax
from jax.experimental import pallas as pl
from jax.experimental.pallas import tpu as pltpu
from jax.sharding import PartitionSpec as P

H = 512
FRONT = 1024
BLOCK = 16
NB = 32
NBF = 64
FD = 32
LEVELS = 4
MESH = pl.DeviceIdType.MESH
HI = lax.Precision.HIGHEST
F32 = jnp.float32


def dot(a, b):
    return jnp.dot(a, b, precision=HI, preferred_element_type=F32)


def dot_tn(a, b):
    return lax.dot_general(
        a, b, (((0,), (0,)), ((), ())), precision=HI, preferred_element_type=F32
    )


def in_three(x):
    high = x.astype(jnp.bfloat16)
    rest = x - high.astype(F32)
    mid = rest.astype(jnp.bfloat16)
    return high, mid, (rest - mid.astype(F32)).astype(jnp.bfloat16)


def outer_sum(left, right):
    h, m, l = in_three(left)
    hh, mm, ll = in_three(right)
    return lax.dot_general(
        jnp.concatenate([h, h, h, m, m, l], 0), jnp.concatenate([hh, mm, ll, hh, mm, hh], 0),
        (((0,), (0,)), ((), ())), preferred_element_type=F32,
    )


def inv128(groups):
    n = len(groups)
    sub = lax.broadcasted_iota(jnp.int32, (8, 128), 0)
    lane = lax.broadcasted_iota(jnp.int32, (8, 128), 1)
    mats = list(groups)

    def lanes_of(x, k):
        return jnp.broadcast_to(x[:, k : k + 1], (8, 128))

    def rows_of(x, k):
        return jnp.broadcast_to(x[k : k + 1, :], (8, 128))

    def update(x, g, rows):
        t = [lanes_of(x, 8 * g + j) * rows[j] for j in range(8)]
        s = ((t[0] + t[1]) + (t[2] + t[3])) + ((t[4] + t[5]) + (t[6] + t[7]))
        return jnp.where((lane >= 8 * g) & (lane < 8 * g + 8), 0.0, x) - s

    cols = [lanes_of(mats[0], k) for k in range(8)]
    for first in range(0, n, 2):
        panel = [first, first + 1]
        near = [i for i in (first + 2, first + 3) if i < n]
        before = [mats[g] for g in panel]
        low, high = 8 * first, 8 * first + 16
        for g in panel:
            h = g + 1 if g + 1 < n else None
            cur = mats[g]
            if h is not None:
                nxt = mats[h]
                over = [lanes_of(cur, 8 * h + k) for k in range(8)]
                coming = [lanes_of(nxt, 8 * h + k) for k in range(8)]
                under = [lanes_of(nxt, 8 * g + k) for k in range(8)]
            for j in range(8):
                e = sub == j
                ln = lane == 8 * g + j
                inv = 1.0 / rows_of(cols[j], j)
                mult = jnp.where(e, inv, -cols[j] * inv)
                row = jnp.where(ln, 1.0, rows_of(cur, j))
                cur = jnp.where(e | ln, 0.0, cur) + mult * row
                spread = [rows_of(cols[k], j) for k in range(j + 1, 8)]
                for k in range(j + 1, 8):
                    cols[k] = jnp.where(e, 0.0, cols[k]) + mult * spread[k - j - 1]
                if h is not None:
                    mult_nxt = -under[j] * inv
                    nxt = jnp.where(ln, 0.0, nxt) + mult_nxt * row
                    for k in range(j + 1, 8):
                        under[k] = under[k] + mult_nxt * spread[k - j - 1]
                    for k in range(8):
                        value = rows_of(over[k], j)
                        coming[k] = coming[k] + mult_nxt * value
                        if j < 7:
                            over[k] = jnp.where(e, 0.0, over[k]) + mult * value
            mats[g] = cur
            rows = [rows_of(cur, j) for j in range(8)]
            if h is not None:
                mats[h] = nxt
                cols = coming
            for i in panel + near:
                if i != g and i != h:
                    mats[i] = update(mats[i], g, rows)
        far = [i for i in range(n) if i not in panel and i not in near]
        sign = jnp.where(lane < low, -1.0, 1.0)
        s = outer_sum(
            jnp.concatenate([x * sign for x in before], 0), jnp.concatenate([mats[g] for g in panel], 0)
        )
        in_panel = (lane >= low) & (lane < high)
        for i in far:
            mats[i] = jnp.where(in_panel, 0.0, mats[i]) - s[8 * i : 8 * i + 8, :]
    return mats


def invert_in_place(o_ref, d_ref, col_ref, r_ref, pumps):
    blocks = H // 128
    d_ref[...] = o_ref[:128, :128]
    col_ref[...] = jnp.zeros_like(col_ref)
    r_ref[...] = jnp.zeros_like(r_ref)

    def step(k, carry):
        for at, pump in enumerate(pumps):
            if pump is not None:
                pl.when(k == at)(pump)
        ks = pl.multiple_of(k * 128, 128)
        after = pl.multiple_of(((k + 1) % blocks) * 128, 128)
        o_ref[...] = o_ref[...] - dot(col_ref[...], r_ref[...])
        diag = jnp.concatenate(inv128([d_ref[8 * i : 8 * i + 8, :] for i in range(16)]), 0)
        rows = dot(diag, o_ref[pl.ds(ks, 128), :])
        col = o_ref[:, pl.ds(ks, 128)]
        row_id = lax.broadcasted_iota(jnp.int32, col.shape, 0)
        col_ref[...] = jnp.where((row_id >= ks) & (row_id < ks + 128), 0.0, col)
        r_ref[...] = rows
        r_ref[:, pl.ds(ks, 128)] = diag
        d_ref[...] = o_ref[pl.ds(after, 128), pl.ds(after, 128)] - dot(
            col_ref[pl.ds(after, 128), :], r_ref[:, pl.ds(after, 128)]
        )
        o_ref[:, pl.ds(ks, 128)] = jnp.zeros((H, 128), F32)
        o_ref[pl.ds(ks, 128), :] = r_ref[...]
        return carry

    lax.fori_loop(0, blocks, step, 0)
    o_ref[...] = o_ref[...] - dot(col_ref[...], r_ref[...])


class Flow:
    def __init__(self, buf, x_first, number, place, sends, recvs):
        self.buf, self.x_first, self.number = buf, x_first, number
        self.place, self.sends, self.recvs = place, sends, recvs
        self.started = []

    def slot(self, back=0):
        _, xi, yi, core = self.place
        if self.x_first:
            return self.buf.at[(xi + 4 - back) % 4, yi, core]
        return self.buf.at[xi, (yi + 4 - back) % 4, core]

    def line(self, back=0, other=False):
        _, xi, yi, core = self.place
        core = 1 - core if other else core
        if self.x_first:
            return self.buf.at[:, (yi + 4 - back) % 4, core]
        return self.buf.at[(xi + 4 - back) % 4, :, core]

    def device(self, along_x, k):
        leaf, xi, yi, core = self.place
        if along_x:
            return (leaf, ((xi + k) % 4) * 8 + yi * 2 + core)
        return (leaf, xi * 8 + ((yi + k) % 4) * 2 + core)

    def sibling(self):
        leaf, xi, yi, core = self.place
        return (leaf, xi * 8 + yi * 2 + 1 - core)

    def copy(self, sem, ref, device):
        return pltpu.make_async_remote_copy(
            src_ref=ref, dst_ref=ref,
            send_sem=self.sends.at[self.number, sem], recv_sem=self.recvs.at[self.number, sem],
            device_id=device, device_id_type=MESH,
        )

    def start(self, *args):
        c = self.copy(*args)
        c.start()

    def put(self, rows):
        _, xi, yi, core = self.place
        self.buf[xi, yi, core] = rows

    def first(self):
        for k in (2, 1, 3):
            self.start(k - 1, self.slot(), self.device(self.x_first, k))

    def second(self):
        for k in (1, 3, 2):
            self.copy(k - 1, self.slot(k), self.device(self.x_first, k)).wait_recv()
        for k in (2, 1, 3):
            self.start(2 + k, self.line(), self.device(not self.x_first, k))
        self.start(6, self.line(), self.sibling())

    def third(self):
        for k in (1, 3, 2):
            self.copy(2 + k, self.line(k), self.device(not self.x_first, k)).wait_recv()
            self.start(6 + k, self.line(k), self.sibling())

    def finish(self):
        for k in (0, 1, 3, 2):
            self.copy(6 + k, self.line(k, True), self.sibling()).wait_recv()
        for k in (1, 2, 3):
            self.copy(k - 1, self.slot(), self.device(self.x_first, k)).wait_send()
            self.copy(2 + k, self.line(), self.device(not self.x_first, k)).wait_send()
        for k in range(4):
            self.copy(6 + k, self.line(k), self.sibling()).wait_send()


def whole(ref):
    return ref[...].reshape(H, H)


def assemble(inv_ref, link, which, s_ref, blocks_ref, zrow_ref, zt_ref, ai_ref, a12_ref, low_ref, me):
    blocks_ref[:NB] = s_ref[...].reshape(NB, BLOCK, H)
    for p in range(NBF):
        zrow_ref[p] = blocks_ref[inv_ref[link, which, p]]
    zt_ref[:NB] = zrow_ref[...].reshape(FRONT, H).T.reshape(NB, BLOCK, FRONT)
    for p in range(NB):
        rows = pl.ds(p * BLOCK, BLOCK)
        block = zt_ref[inv_ref[link, which, p]]
        ai_ref[rows, :] = ai_ref[rows, :] + block[:, :H]
        a12_ref[rows, :] = a12_ref[rows, :] + block[:, H:]
    low_ref[...] = low_ref[...] + zt_ref[inv_ref[link, which, NB + me]]


def main_kernel(inv_ref, map_ref, leaf_ref, upper_ref, cov_ref, out_ref, *scratch):
    scratch = list(scratch)

    def take(n):
        got = scratch[:n]
        del scratch[:n]
        return got

    g11, g12, s_own, s_par = take(4), take(4), take(3), take(3)
    (gcov,) = take(1)
    ai, a12, gts, xts = take(4), take(4), take(4), take(4)
    blocks, zrow, zt, low, zt_up, rt, yt_ref, diag, col, row, sends, recvs, z_sems = scratch
    blocks[NB] = jnp.zeros((BLOCK, H), F32)
    zt[NB] = jnp.zeros((BLOCK, FRONT), F32)
    for xt_ref in xts:
        xt_ref[NB] = jnp.zeros((BLOCK, 2 * BLOCK), F32)

    leaf = lax.axis_index("leaf")
    me = lax.axis_index("front")
    xi, yi, core = me // 8, (me // 2) % 4, me % 2
    place = (leaf, xi, yi, core)
    across_to = [(leaf + d - 2 * d * ((leaf // d) % 2), me) for d in (1, 2, 4)]
    partners = [(leaf, ((xi + k) % 4) * 8 + yi * 2 + core) for k in (1, 2, 3)]
    partners += [(leaf, xi * 8 + ((yi + k) % 4) * 2 + core) for k in (1, 2, 3)]
    partners += [(leaf, me + 1 - 2 * core)] + across_to
    barrier = pltpu.get_barrier_semaphore()
    for device in partners:
        pl.semaphore_signal(barrier, inc=1, device_id=device, device_id_type=MESH)

    numbers = iter(range(15))
    front_flows = [
        (Flow(g11[h], True, next(numbers), place, sends, recvs), Flow(g12[h], False, next(numbers), place, sends, recvs))
        for h in range(LEVELS)
    ]
    cov_flow = Flow(gcov, True, next(numbers), place, sends, recvs)
    schur_flows = [
        (Flow(s_own[h], True, next(numbers), place, sends, recvs), Flow(s_par[h], False, next(numbers), place, sends, recvs))
        for h in range(LEVELS - 1)
    ]
    nodes = [None, leaf // 2, 4 + leaf // 4, 6]

    def open_flows(height):
        if height == 0:
            front_flows[0][0].put(leaf_ref[0, 0, :, :H])
            front_flows[0][1].put(leaf_ref[0, 0, :, H:])
        else:
            front_flows[height][0].put(upper_ref[nodes[height], 0, :, :H])
            front_flows[height][1].put(upper_ref[nodes[height], 0, :, H:])
        for flow in front_flows[height]:
            flow.first()

    def pumps(flows, opening):
        def second():
            for flow in flows:
                flow.second()

        def third():
            for flow in flows:
                flow.third()

        def finish():
            for flow in flows:
                flow.finish()

        return (opening, second, third, finish)

    front_flows[0][0].put(leaf_ref[0, 0, :, :H])
    front_flows[0][1].put(leaf_ref[0, 0, :, H:])
    pl.semaphore_wait(barrier, len(partners))
    for flow in front_flows[0]:
        flow.first()
    for flow in front_flows[0]:
        flow.second()
    for flow in front_flows[0]:
        flow.third()
    front_flows[0][0].finish()
    ai[0][...] = whole(g11[0])
    front_flows[0][1].finish()
    a12[0][...] = whole(g12[0])
    low[...] = leaf_ref[0, 1]

    for height in range(LEVELS):
        last = height == LEVELS - 1
        if height > 0:
            ai[height][...] = whole(g11[height])
            a12[height][...] = whole(g12[height])
            low[...] = upper_ref[nodes[height], 1]
            for which, (flow, s_ref) in enumerate(zip(schur_flows[height - 1], (s_own[height - 1], s_par[height - 1]))):
                flow.finish()
                assemble(inv_ref, height - 1, which, s_ref, blocks, zrow, zt, ai[height], a12[height], low, me)
        if last:
            def opening():
                cov_flow.put(cov_ref[...])
                cov_flow.first()

            invert_in_place(ai[height], diag, col, row, pumps([cov_flow], opening))
        else:
            def opening(above=height + 1):
                open_flows(above)

            invert_in_place(ai[height], diag, col, row, pumps(front_flows[height + 1], opening))
            own_flow, par_flow = schur_flows[height]
            g = dot(low[:, :H], ai[height][...])
            own_flow.put(low[:, H:] - dot(g, a12[height][...]))
            across = pltpu.make_async_remote_copy(
                src_ref=s_own[height].at[xi, yi, core], dst_ref=s_par[height].at[xi, yi, core],
                send_sem=z_sems.at[height, 0], recv_sem=z_sems.at[height, 1],
                device_id=across_to[height], device_id_type=MESH,
            )
            across.start()
            own_flow.first()
        if height == 0:
            rows = lax.broadcasted_iota(jnp.int32, (H, 2 * BLOCK), 0)
            cols = lax.broadcasted_iota(jnp.int32, (H, 2 * BLOCK), 1)
            za = ((rows == me * BLOCK + cols) & (cols < BLOCK)).astype(F32)
            zb = ((rows == (me - 1) * BLOCK + cols) & (cols >= BLOCK)).astype(F32)
        else:
            for p in range(NBF):
                zt_up[pl.ds(p * BLOCK, BLOCK), :] = xts[height - 1][inv_ref[height - 1, 0, p]]
            za, zb = zt_up[:H, :], zt_up[H:, :]
        gt = dot(ai[height][...], za)
        gts[height][...] = gt
        xt = zb - dot_tn(a12[height][...], gt)
        xts[height][:NB] = xt.reshape(NB, BLOCK, 2 * BLOCK)
        if not last:
            across.wait_recv()
            par_flow.first()
            own_flow.second()
            par_flow.second()
            own_flow.third()
            par_flow.third()
            across.wait_send()

    yt_ref[...] = dot(whole(gcov), xt)
    for height in range(LEVELS - 1, -1, -1):
        yt = yt_ref[...]
        top = gts[height][...] - dot(ai[height][...], dot(a12[height][...], yt))
        rt[:NB] = top.reshape(NB, BLOCK, 2 * BLOCK)
        rt[NB:] = yt.reshape(NB, BLOCK, 2 * BLOCK)
        if height > 0:
            for a in range(NB):
                yt_ref[pl.ds(a * BLOCK, BLOCK), :] = rt[map_ref[height - 1, a]]
    out_ref[...] = rt[...].reshape(FRONT, 2 * BLOCK).T.reshape(1, 2, BLOCK, FRONT)


def body(fronts_leaf, fronts_upper, block_map, parent_cov):
    leaves = 8
    my_leaf = lax.axis_index("leaf")
    own_index = []
    for height in range(1, LEVELS):
        child = jnp.right_shift(my_leaf, height - 1)
        own_index.append(2 * leaves - 4 * leaves // 2**height + child)
    index = jnp.stack([jnp.stack([i, jnp.bitwise_xor(i, 1)]) for i in own_index])
    maps = block_map[index]
    hit = maps[:, :, None, :] == jnp.arange(NBF, dtype=jnp.int32)[None, None, :, None]
    where_from = jnp.arange(NB, dtype=jnp.int32) - NB
    inverse_maps = NB + jnp.sum(jnp.where(hit, where_from, 0), -1, dtype=jnp.int32)
    vm = pl.BlockSpec(memory_space=pltpu.VMEM)
    sm = pl.BlockSpec(memory_space=pltpu.SMEM)
    plane = pltpu.VMEM((4, 4, 2, BLOCK, H), F32)
    square = pltpu.VMEM((H, H), F32)
    thin = pltpu.VMEM((H, 2 * BLOCK), F32)
    parts = pltpu.VMEM((NB + 1, BLOCK, 2 * BLOCK), F32)
    sems = pltpu.SemaphoreType.DMA
    return pl.pallas_call(
        main_kernel,
        out_shape=jax.ShapeDtypeStruct((1, 2, BLOCK, FRONT), F32),
        in_specs=[sm, sm, vm, vm, vm],
        out_specs=vm,
        scratch_shapes=[plane] * 15 + [square] * 8 + [thin] * 4 + [parts] * 4
        + [
            pltpu.VMEM((NB + 1, BLOCK, H), F32),
            pltpu.VMEM((NBF, BLOCK, H), F32),
            pltpu.VMEM((NB + 1, BLOCK, FRONT), F32),
            pltpu.VMEM((BLOCK, FRONT), F32),
            pltpu.VMEM((FRONT, 2 * BLOCK), F32),
            pltpu.VMEM((NBF, BLOCK, 2 * BLOCK), F32),
            pltpu.VMEM((H, 2 * BLOCK), F32),
            pltpu.VMEM((128, 128), F32),
            pltpu.VMEM((H, 128), F32),
            pltpu.VMEM((128, H), F32),
            sems((15, 10)), sems((15, 10)), sems((3, 2)),
        ],
        compiler_params=pltpu.CompilerParams(
            collective_id=0, has_side_effects=True, vmem_limit_bytes=56 * 2**20
        ),
    )(inverse_maps, maps[:, 0], fronts_leaf, fronts_upper, parent_cov)


def solution(mesh):
    placed = (P("leaf", None, "front", None), P(None, None, "front", None), P(), P("front", None))
    return jax.shard_map(
        body, mesh=mesh, in_specs=placed, out_specs=P("leaf", None, "front", None), check_vma=False
    )
```

```python
import jax
import jax.numpy as jnp
from jax import lax
from jax.experimental import pallas as pl
from jax.experimental.pallas import tpu as pltpu
from jax.sharding import PartitionSpec as P

H = 512
FRONT = 1024
BLOCK = 16
NB = 32
NBF = 64
FD = 32
LEVELS = 4
MESH = pl.DeviceIdType.MESH
HI = lax.Precision.HIGHEST
F32 = jnp.float32


def dot(a, b):
    return jnp.dot(a, b, precision=HI, preferred_element_type=F32)


def dot_tn(a, b):
    return lax.dot_general(
        a, b, (((0,), (0,)), ((), ())), precision=HI, preferred_element_type=F32
    )


def in_three(x):
    high = x.astype(jnp.bfloat16)
    rest = x - high.astype(F32)
    mid = rest.astype(jnp.bfloat16)
    return high, mid, (rest - mid.astype(F32)).astype(jnp.bfloat16)


def outer_sum(left, right):
    h, m, l = in_three(left)
    hh, mm, ll = in_three(right)
    return lax.dot_general(
        jnp.concatenate([h, h, h, m, m, l], 0), jnp.concatenate([hh, mm, ll, hh, mm, hh], 0),
        (((0,), (0,)), ((), ())), preferred_element_type=F32,
    )


def inv128(groups):
    n = len(groups)
    sub = lax.broadcasted_iota(jnp.int32, (8, 128), 0)
    lane = lax.broadcasted_iota(jnp.int32, (8, 128), 1)
    mats = list(groups)

    def lanes_of(x, k):
        return jnp.broadcast_to(x[:, k : k + 1], (8, 128))

    def rows_of(x, k):
        return jnp.broadcast_to(x[k : k + 1, :], (8, 128))

    def update(x, g, rows):
        t = [lanes_of(x, 8 * g + j) * rows[j] for j in range(8)]
        s = ((t[0] + t[1]) + (t[2] + t[3])) + ((t[4] + t[5]) + (t[6] + t[7]))
        return jnp.where((lane >= 8 * g) & (lane < 8 * g + 8), 0.0, x) - s

    cols = [lanes_of(mats[0], k) for k in range(8)]
    for first in range(0, n, 2):
        panel = [first, first + 1]
        near = [i for i in (first + 2, first + 3) if i < n]
        before = [mats[g] for g in panel]
        low, high = 8 * first, 8 * first + 16
        for g in panel:
            h = g + 1 if g + 1 < n else None
            cur = mats[g]
            if h is not None:
                nxt = mats[h]
                over = [lanes_of(cur, 8 * h + k) for k in range(8)]
                coming = [lanes_of(nxt, 8 * h + k) for k in range(8)]
                under = [lanes_of(nxt, 8 * g + k) for k in range(8)]
            for j in range(8):
                e = sub == j
                ln = lane == 8 * g + j
                inv = 1.0 / rows_of(cols[j], j)
                mult = jnp.where(e, inv, -cols[j] * inv)
                row = jnp.where(ln, 1.0, rows_of(cur, j))
                cur = jnp.where(e | ln, 0.0, cur) + mult * row
                spread = [rows_of(cols[k], j) for k in range(j + 1, 8)]
                for k in range(j + 1, 8):
                    cols[k] = jnp.where(e, 0.0, cols[k]) + mult * spread[k - j - 1]
                if h is not None:
                    mult_nxt = -under[j] * inv
                    nxt = jnp.where(ln, 0.0, nxt) + mult_nxt * row
                    for k in range(j + 1, 8):
                        under[k] = under[k] + mult_nxt * spread[k - j - 1]
                    for k in range(8):
                        value = rows_of(over[k], j)
                        coming[k] = coming[k] + mult_nxt * value
                        if j < 7:
                            over[k] = jnp.where(e, 0.0, over[k]) + mult * value
            mats[g] = cur
            rows = [rows_of(cur, j) for j in range(8)]
            if h is not None:
                mats[h] = nxt
                cols = coming
            for i in panel + near:
                if i != g and i != h:
                    mats[i] = update(mats[i], g, rows)
        far = [i for i in range(n) if i not in panel and i not in near]
        sign = jnp.where(lane < low, -1.0, 1.0)
        s = outer_sum(
            jnp.concatenate([x * sign for x in before], 0), jnp.concatenate([mats[g] for g in panel], 0)
        )
        in_panel = (lane >= low) & (lane < high)
        for i in far:
            mats[i] = jnp.where(in_panel, 0.0, mats[i]) - s[8 * i : 8 * i + 8, :]
    return mats


def invert_in_place(o_ref, d_ref, col_ref, r_ref, pumps):
    blocks = H // 128
    d_ref[...] = o_ref[:128, :128]
    col_ref[...] = jnp.zeros_like(col_ref)
    r_ref[...] = jnp.zeros_like(r_ref)

    def step(k, carry):
        for at, pump in enumerate(pumps):
            if pump is not None:
                pl.when(k == at)(pump)
        ks = pl.multiple_of(k * 128, 128)
        after = pl.multiple_of(((k + 1) % blocks) * 128, 128)
        o_ref[...] = o_ref[...] - dot(col_ref[...], r_ref[...])
        diag = jnp.concatenate(inv128([d_ref[8 * i : 8 * i + 8, :] for i in range(16)]), 0)
        rows = dot(diag, o_ref[pl.ds(ks, 128), :])
        col = o_ref[:, pl.ds(ks, 128)]
        row_id = lax.broadcasted_iota(jnp.int32, col.shape, 0)
        col_ref[...] = jnp.where((row_id >= ks) & (row_id < ks + 128), 0.0, col)
        r_ref[...] = rows
        r_ref[:, pl.ds(ks, 128)] = diag
        d_ref[...] = o_ref[pl.ds(after, 128), pl.ds(after, 128)] - dot(
            col_ref[pl.ds(after, 128), :], r_ref[:, pl.ds(after, 128)]
        )
        o_ref[:, pl.ds(ks, 128)] = jnp.zeros((H, 128), F32)
        o_ref[pl.ds(ks, 128), :] = r_ref[...]
        return carry

    lax.fori_loop(0, blocks, step, 0)
    o_ref[...] = o_ref[...] - dot(col_ref[...], r_ref[...])


class Flow:
    def __init__(self, buf, x_first, number, place, sends, recvs):
        self.buf, self.x_first, self.number = buf, x_first, number
        self.place, self.sends, self.recvs = place, sends, recvs
        self.started = []

    def slot(self, back=0):
        _, xi, yi, core = self.place
        if self.x_first:
            return self.buf.at[(xi + 4 - back) % 4, yi, core]
        return self.buf.at[xi, (yi + 4 - back) % 4, core]

    def line(self, back=0, other=False):
        _, xi, yi, core = self.place
        core = 1 - core if other else core
        if self.x_first:
            return self.buf.at[:, (yi + 4 - back) % 4, core]
        return self.buf.at[(xi + 4 - back) % 4, :, core]

    def device(self, along_x, k):
        leaf, xi, yi, core = self.place
        if along_x:
            return (leaf, ((xi + k) % 4) * 8 + yi * 2 + core)
        return (leaf, xi * 8 + ((yi + k) % 4) * 2 + core)

    def sibling(self):
        leaf, xi, yi, core = self.place
        return (leaf, xi * 8 + yi * 2 + 1 - core)

    def copy(self, sem, ref, device):
        return pltpu.make_async_remote_copy(
            src_ref=ref, dst_ref=ref,
            send_sem=self.sends.at[self.number, sem], recv_sem=self.recvs.at[self.number, sem],
            device_id=device, device_id_type=MESH,
        )

    def start(self, *args):
        c = self.copy(*args)
        c.start()

    def put(self, rows):
        _, xi, yi, core = self.place
        self.buf[xi, yi, core] = rows

    def first(self):
        for k in (2, 1, 3):
            self.start(k - 1, self.slot(), self.device(self.x_first, k))

    def second(self):
        for k in (1, 3, 2):
            self.copy(k - 1, self.slot(k), self.device(self.x_first, k)).wait_recv()
        for k in (2, 1, 3):
            self.start(2 + k, self.line(), self.device(not self.x_first, k))
        self.start(6, self.line(), self.sibling())

    def third(self):
        for k in (1, 3, 2):
            self.copy(2 + k, self.line(k), self.device(not self.x_first, k)).wait_recv()
            self.start(6 + k, self.line(k), self.sibling())

    def finish(self):
        for k in (0, 1, 3, 2):
            self.copy(6 + k, self.line(k, True), self.sibling()).wait_recv()
        for k in (1, 2, 3):
            self.copy(k - 1, self.slot(), self.device(self.x_first, k)).wait_send()
            self.copy(2 + k, self.line(), self.device(not self.x_first, k)).wait_send()
        for k in range(4):
            self.copy(6 + k, self.line(k), self.sibling()).wait_send()


class EagerFlow(Flow):
    def at(self, b, k=0):
        _, xi, yi, core = self.place
        if self.x_first:
            return self.buf.at[(xi + 4 - b) % 4, (yi + 4 - k) % 4, core]
        return self.buf.at[(xi + 4 - k) % 4, (yi + 4 - b) % 4, core]

    def first(self):
        for k in (2, 1, 3):
            self.start(k - 1, self.at(0), self.device(self.x_first, k))
        for k in (2, 1, 3):
            self.start(2 + k, self.at(0), self.device(not self.x_first, k))

    def second(self):
        for b in (1, 3, 2):
            self.copy(b - 1, self.at(b), self.device(self.x_first, b)).wait_recv()
            for k in (2, 1, 3):
                self.start(2 + 3 * b + k, self.at(b), self.device(not self.x_first, k))
        self.start(15, self.line(), self.sibling())

    def third(self):
        for k in (1, 3, 2):
            for b in range(4):
                self.copy(2 + 3 * b + k, self.at(b, k), self.device(not self.x_first, k)).wait_recv()
            self.start(15 + k, self.line(k), self.sibling())

    def finish(self):
        for k in (0, 1, 3, 2):
            self.copy(15 + k, self.line(k, True), self.sibling()).wait_recv()
        for k in (1, 2, 3):
            self.copy(k - 1, self.at(0), self.device(self.x_first, k)).wait_send()
            for b in range(4):
                self.copy(2 + 3 * b + k, self.at(b), self.device(not self.x_first, k)).wait_send()
        for k in range(4):
            self.copy(15 + k, self.line(k), self.sibling()).wait_send()


def whole(ref):
    return ref[...].reshape(H, H)


def spread(inv_ref, link, which, s_ref, blocks_ref, zrow_ref, zt_ref):
    blocks_ref[:NB] = s_ref[...].reshape(NB, BLOCK, H)
    for p in range(NBF):
        zrow_ref[p] = blocks_ref[inv_ref[link, which, p]]
    zt_ref[:NB] = zrow_ref[...].reshape(FRONT, H).T.reshape(NB, BLOCK, FRONT)


def add_rows(inv_ref, link, which, zt_ref, ai_ref, a12_ref, low_ref, me):
    for p in range(NB):
        rows = pl.ds(p * BLOCK, BLOCK)
        block = zt_ref[inv_ref[link, which, p]]
        ai_ref[rows, :] = ai_ref[rows, :] + block[:, :H]
        a12_ref[rows, :] = a12_ref[rows, :] + block[:, H:]
    low_ref[...] = low_ref[...] + zt_ref[inv_ref[link, which, NB + me]]


def main_kernel(inv_ref, map_ref, leaf_ref, upper_ref, cov_ref, out_ref, *scratch):
    scratch = list(scratch)

    def take(n):
        got = scratch[:n]
        del scratch[:n]
        return got

    g11, g12, s_own, s_par = take(4), take(4), take(3), take(3)
    (gcov,) = take(1)
    ai, a12, gts, xts = take(4), take(4), take(4), take(4)
    blocks, zrow, zt, low, zt_up, rt, yt_ref, diag, col, row, sends, recvs, eager_sends, eager_recvs, z_sems = scratch
    blocks[NB] = jnp.zeros((BLOCK, H), F32)
    zt[NB] = jnp.zeros((BLOCK, FRONT), F32)
    for xt_ref in xts:
        xt_ref[NB] = jnp.zeros((BLOCK, 2 * BLOCK), F32)

    leaf = lax.axis_index("leaf")
    me = lax.axis_index("front")
    xi, yi, core = me // 8, (me // 2) % 4, me % 2
    place = (leaf, xi, yi, core)
    across_to = [(leaf + d - 2 * d * ((leaf // d) % 2), me) for d in (1, 2, 4)]
    partners = [(leaf, ((xi + k) % 4) * 8 + yi * 2 + core) for k in (1, 2, 3)]
    partners += [(leaf, xi * 8 + ((yi + k) % 4) * 2 + core) for k in (1, 2, 3)]
    partners += [(leaf, me + 1 - 2 * core)] + across_to
    barrier = pltpu.get_barrier_semaphore()
    for device in partners:
        pl.semaphore_signal(barrier, inc=1, device_id=device, device_id_type=MESH)

    def eager(buf, x_first, number):
        return EagerFlow(buf, x_first, number, place, eager_sends, eager_recvs)

    def lazy(buf, x_first, number):
        return Flow(buf, x_first, number, place, sends, recvs)

    front_flows = [(eager(g11[0], True, 0), eager(g12[0], False, 1))]
    front_flows += [
        (lazy(g11[h], True, 2 * h - 2), lazy(g12[h], False, 2 * h - 1)) for h in range(1, LEVELS)
    ]
    cov_flow = lazy(gcov, True, 6)
    schur_flows = [
        (eager(s_own[h], True, 2 * h + 2), eager(s_par[h], False, 2 * h + 3)) for h in range(LEVELS - 1)
    ]
    nodes = [None, leaf // 2, 4 + leaf // 4, 6]

    def open_flows(height):
        front_flows[height][0].put(upper_ref[nodes[height], 0, :, :H])
        front_flows[height][1].put(upper_ref[nodes[height], 0, :, H:])
        for flow in front_flows[height]:
            flow.first()

    def pumps(flows, opening):
        def second():
            for flow in flows:
                flow.second()

        def third():
            for flow in flows:
                flow.third()

        def finish():
            for flow in flows:
                flow.finish()

        return (opening, second, third, finish)

    front_flows[0][0].put(leaf_ref[0, 0, :, :H])
    front_flows[0][1].put(leaf_ref[0, 0, :, H:])
    pl.semaphore_wait(barrier, len(partners))
    for flow in front_flows[0]:
        flow.first()
    for flow in front_flows[0]:
        flow.second()
    for flow in front_flows[0]:
        flow.third()
    front_flows[0][0].finish()
    ai[0][...] = whole(g11[0])
    front_flows[0][1].finish()
    a12[0][...] = whole(g12[0])
    low[...] = leaf_ref[0, 1]

    for height in range(LEVELS):
        last = height == LEVELS - 1
        if height > 0:
            ai[height][...] = whole(g11[height])
            a12[height][...] = whole(g12[height])
            low[...] = upper_ref[nodes[height], 1]
            link = height - 1
            own_flow, par_flow = schur_flows[link]
            own_flow.finish()
            spread(inv_ref, link, 0, s_own[link], blocks, zrow, zt)
            par_flow.third()
            add_rows(inv_ref, link, 0, zt, ai[height], a12[height], low, me)
            par_flow.finish()
            spread(inv_ref, link, 1, s_par[link], blocks, zrow, zt)
            add_rows(inv_ref, link, 1, zt, ai[height], a12[height], low, me)
        if last:
            def opening():
                cov_flow.put(cov_ref[...])
                cov_flow.first()

            invert_in_place(ai[height], diag, col, row, pumps([cov_flow], opening))
        else:
            def opening(above=height + 1):
                open_flows(above)

            invert_in_place(ai[height], diag, col, row, pumps(front_flows[height + 1], opening))
            own_flow, par_flow = schur_flows[height]
            g = dot(low[:, :H], ai[height][...])
            own_flow.put(low[:, H:] - dot(g, a12[height][...]))
            across = pltpu.make_async_remote_copy(
                src_ref=s_own[height].at[xi, yi, core], dst_ref=s_par[height].at[xi, yi, core],
                send_sem=z_sems.at[height, 0], recv_sem=z_sems.at[height, 1],
                device_id=across_to[height], device_id_type=MESH,
            )
            across.start()
            own_flow.first()
        if height == 0:
            rows = lax.broadcasted_iota(jnp.int32, (H, 2 * BLOCK), 0)
            cols = lax.broadcasted_iota(jnp.int32, (H, 2 * BLOCK), 1)
            za = ((rows == me * BLOCK + cols) & (cols < BLOCK)).astype(F32)
            zb = ((rows == (me - 1) * BLOCK + cols) & (cols >= BLOCK)).astype(F32)
        else:
            for p in range(NBF):
                zt_up[pl.ds(p * BLOCK, BLOCK), :] = xts[height - 1][inv_ref[height - 1, 0, p]]
            za, zb = zt_up[:H, :], zt_up[H:, :]
        gt = dot(ai[height][...], za)
        gts[height][...] = gt
        xt = zb - dot_tn(a12[height][...], gt)
        xts[height][:NB] = xt.reshape(NB, BLOCK, 2 * BLOCK)
        if not last:
            across.wait_recv()
            par_flow.first()
            own_flow.second()
            par_flow.second()
            own_flow.third()
            across.wait_send()

    yt_ref[...] = dot(whole(gcov), xt)
    for height in range(LEVELS - 1, -1, -1):
        yt = yt_ref[...]
        top = gts[height][...] - dot(ai[height][...], dot(a12[height][...], yt))
        rt[:NB] = top.reshape(NB, BLOCK, 2 * BLOCK)
        rt[NB:] = yt.reshape(NB, BLOCK, 2 * BLOCK)
        if height > 0:
            for a in range(NB):
                yt_ref[pl.ds(a * BLOCK, BLOCK), :] = rt[map_ref[height - 1, a]]
    out_ref[...] = rt[...].reshape(FRONT, 2 * BLOCK).T.reshape(1, 2, BLOCK, FRONT)


def body(fronts_leaf, fronts_upper, block_map, parent_cov):
    leaves = 8
    my_leaf = lax.axis_index("leaf")
    own_index = []
    for height in range(1, LEVELS):
        child = jnp.right_shift(my_leaf, height - 1)
        own_index.append(2 * leaves - 4 * leaves // 2**height + child)
    index = jnp.stack([jnp.stack([i, jnp.bitwise_xor(i, 1)]) for i in own_index])
    maps = block_map[index]
    hit = maps[:, :, None, :] == jnp.arange(NBF, dtype=jnp.int32)[None, None, :, None]
    where_from = jnp.arange(NB, dtype=jnp.int32) - NB
    inverse_maps = NB + jnp.sum(jnp.where(hit, where_from, 0), -1, dtype=jnp.int32)
    vm = pl.BlockSpec(memory_space=pltpu.VMEM)
    sm = pl.BlockSpec(memory_space=pltpu.SMEM)
    plane = pltpu.VMEM((4, 4, 2, BLOCK, H), F32)
    square = pltpu.VMEM((H, H), F32)
    thin = pltpu.VMEM((H, 2 * BLOCK), F32)
    parts = pltpu.VMEM((NB + 1, BLOCK, 2 * BLOCK), F32)
    sems = pltpu.SemaphoreType.DMA
    return pl.pallas_call(
        main_kernel,
        out_shape=jax.ShapeDtypeStruct((1, 2, BLOCK, FRONT), F32),
        in_specs=[sm, sm, vm, vm, vm],
        out_specs=vm,
        scratch_shapes=[plane] * 15 + [square] * 8 + [thin] * 4 + [parts] * 4
        + [
            pltpu.VMEM((NB + 1, BLOCK, H), F32),
            pltpu.VMEM((NBF, BLOCK, H), F32),
            pltpu.VMEM((NB + 1, BLOCK, FRONT), F32),
            pltpu.VMEM((BLOCK, FRONT), F32),
            pltpu.VMEM((FRONT, 2 * BLOCK), F32),
            pltpu.VMEM((NBF, BLOCK, 2 * BLOCK), F32),
            pltpu.VMEM((H, 2 * BLOCK), F32),
            pltpu.VMEM((128, 128), F32),
            pltpu.VMEM((H, 128), F32),
            pltpu.VMEM((128, H), F32),
            sems((7, 10)), sems((7, 10)), sems((8, 19)), sems((8, 19)), sems((3, 2)),
        ],
        compiler_params=pltpu.CompilerParams(
            collective_id=0, has_side_effects=True, vmem_limit_bytes=56 * 2**20
        ),
    )(inverse_maps, maps[:, 0], fronts_leaf, fronts_upper, parent_cov)


def solution(mesh):
    placed = (P("leaf", None, "front", None), P(None, None, "front", None), P(), P("front", None))
    return jax.shard_map(
        body, mesh=mesh, in_specs=placed, out_specs=P("leaf", None, "front", None), check_vma=False
    )
```

```python
import jax
import jax.numpy as jnp
from jax import lax
from jax.experimental import pallas as pl
from jax.experimental.pallas import tpu as pltpu
from jax.sharding import PartitionSpec as P

H = 512
FRONT = 1024
BLOCK = 16
NB = 32
NBF = 64
FD = 32
LEVELS = 4
MESH = pl.DeviceIdType.MESH
HI = lax.Precision.HIGHEST
F32 = jnp.float32


def dot(a, b):
    return jnp.dot(a, b, precision=HI, preferred_element_type=F32)


def dot_tn(a, b):
    return lax.dot_general(
        a, b, (((0,), (0,)), ((), ())), precision=HI, preferred_element_type=F32
    )


def in_three(x):
    high = x.astype(jnp.bfloat16)
    rest = x - high.astype(F32)
    mid = rest.astype(jnp.bfloat16)
    return high, mid, (rest - mid.astype(F32)).astype(jnp.bfloat16)


def outer_sum(left, right):
    h, m, l = in_three(left)
    hh, mm, ll = in_three(right)
    return lax.dot_general(
        jnp.concatenate([h, h, h, m, m, l], 0), jnp.concatenate([hh, mm, ll, hh, mm, hh], 0),
        (((0,), (0,)), ((), ())), preferred_element_type=F32,
    )


def inv128(groups):
    n = len(groups)
    sub = lax.broadcasted_iota(jnp.int32, (8, 128), 0)
    lane = lax.broadcasted_iota(jnp.int32, (8, 128), 1)
    mats = list(groups)

    def lanes_of(x, k):
        return jnp.broadcast_to(x[:, k : k + 1], (8, 128))

    def rows_of(x, k):
        return jnp.broadcast_to(x[k : k + 1, :], (8, 128))

    def update(x, g, rows):
        t = [lanes_of(x, 8 * g + j) * rows[j] for j in range(8)]
        s = ((t[0] + t[1]) + (t[2] + t[3])) + ((t[4] + t[5]) + (t[6] + t[7]))
        return jnp.where((lane >= 8 * g) & (lane < 8 * g + 8), 0.0, x) - s

    cols = [lanes_of(mats[0], k) for k in range(8)]
    for first in range(0, n, 2):
        panel = [first, first + 1]
        near = [i for i in (first + 2, first + 3) if i < n]
        before = [mats[g] for g in panel]
        low, high = 8 * first, 8 * first + 16
        for g in panel:
            h = g + 1 if g + 1 < n else None
            cur = mats[g]
            if h is not None:
                nxt = mats[h]
                over = [lanes_of(cur, 8 * h + k) for k in range(8)]
                coming = [lanes_of(nxt, 8 * h + k) for k in range(8)]
                under = [lanes_of(nxt, 8 * g + k) for k in range(8)]
            for j in range(8):
                e = sub == j
                ln = lane == 8 * g + j
                inv = 1.0 / rows_of(cols[j], j)
                mult = jnp.where(e, inv, -cols[j] * inv)
                row = jnp.where(ln, 1.0, rows_of(cur, j))
                cur = jnp.where(e | ln, 0.0, cur) + mult * row
                spread = [rows_of(cols[k], j) for k in range(j + 1, 8)]
                for k in range(j + 1, 8):
                    cols[k] = jnp.where(e, 0.0, cols[k]) + mult * spread[k - j - 1]
                if h is not None:
                    mult_nxt = -under[j] * inv
                    nxt = jnp.where(ln, 0.0, nxt) + mult_nxt * row
                    for k in range(j + 1, 8):
                        under[k] = under[k] + mult_nxt * spread[k - j - 1]
                    for k in range(8):
                        value = rows_of(over[k], j)
                        coming[k] = coming[k] + mult_nxt * value
                        if j < 7:
                            over[k] = jnp.where(e, 0.0, over[k]) + mult * value
            mats[g] = cur
            rows = [rows_of(cur, j) for j in range(8)]
            if h is not None:
                mats[h] = nxt
                cols = coming
            for i in panel + near:
                if i != g and i != h:
                    mats[i] = update(mats[i], g, rows)
        far = [i for i in range(n) if i not in panel and i not in near]
        sign = jnp.where(lane < low, -1.0, 1.0)
        s = outer_sum(
            jnp.concatenate([x * sign for x in before], 0), jnp.concatenate([mats[g] for g in panel], 0)
        )
        in_panel = (lane >= low) & (lane < high)
        for i in far:
            mats[i] = jnp.where(in_panel, 0.0, mats[i]) - s[8 * i : 8 * i + 8, :]
    return mats


def invert_in_place(o_ref, d_ref, col_ref, r_ref, pumps):
    blocks = H // 128
    d_ref[...] = o_ref[:128, :128]
    col_ref[...] = jnp.zeros_like(col_ref)
    r_ref[...] = jnp.zeros_like(r_ref)

    def step(k, carry):
        for at, pump in enumerate(pumps):
            if pump is not None:
                pl.when(k == at)(pump)
        ks = pl.multiple_of(k * 128, 128)
        after = pl.multiple_of(((k + 1) % blocks) * 128, 128)
        o_ref[...] = o_ref[...] - dot(col_ref[...], r_ref[...])
        diag = jnp.concatenate(inv128([d_ref[8 * i : 8 * i + 8, :] for i in range(16)]), 0)
        rows = dot(diag, o_ref[pl.ds(ks, 128), :])
        col = o_ref[:, pl.ds(ks, 128)]
        row_id = lax.broadcasted_iota(jnp.int32, col.shape, 0)
        col_ref[...] = jnp.where((row_id >= ks) & (row_id < ks + 128), 0.0, col)
        r_ref[...] = rows
        r_ref[:, pl.ds(ks, 128)] = diag
        d_ref[...] = o_ref[pl.ds(after, 128), pl.ds(after, 128)] - dot(
            col_ref[pl.ds(after, 128), :], r_ref[:, pl.ds(after, 128)]
        )
        o_ref[:, pl.ds(ks, 128)] = jnp.zeros((H, 128), F32)
        o_ref[pl.ds(ks, 128), :] = r_ref[...]
        return carry

    lax.fori_loop(0, blocks, step, 0)
    o_ref[...] = o_ref[...] - dot(col_ref[...], r_ref[...])


class Flow:
    def __init__(self, buf, x_first, number, place, sends, recvs):
        self.buf, self.x_first, self.number = buf, x_first, number
        self.place, self.sends, self.recvs = place, sends, recvs
        self.started = []

    def slot(self, back=0):
        _, xi, yi, core = self.place
        if self.x_first:
            return self.buf.at[(xi + 4 - back) % 4, yi, core]
        return self.buf.at[xi, (yi + 4 - back) % 4, core]

    def line(self, back=0, other=False):
        _, xi, yi, core = self.place
        core = 1 - core if other else core
        if self.x_first:
            return self.buf.at[:, (yi + 4 - back) % 4, core]
        return self.buf.at[(xi + 4 - back) % 4, :, core]

    def device(self, along_x, k):
        leaf, xi, yi, core = self.place
        if along_x:
            return (leaf, ((xi + k) % 4) * 8 + yi * 2 + core)
        return (leaf, xi * 8 + ((yi + k) % 4) * 2 + core)

    def sibling(self):
        leaf, xi, yi, core = self.place
        return (leaf, xi * 8 + yi * 2 + 1 - core)

    def copy(self, sem, ref, device):
        return pltpu.make_async_remote_copy(
            src_ref=ref, dst_ref=ref,
            send_sem=self.sends.at[self.number, sem], recv_sem=self.recvs.at[self.number, sem],
            device_id=device, device_id_type=MESH,
        )

    def start(self, *args):
        c = self.copy(*args)
        c.start()

    def put(self, rows):
        _, xi, yi, core = self.place
        self.buf[xi, yi, core] = rows

    def first(self):
        for k in (2, 1, 3):
            self.start(k - 1, self.slot(), self.device(self.x_first, k))

    def second(self):
        for k in (1, 3, 2):
            self.copy(k - 1, self.slot(k), self.device(self.x_first, k)).wait_recv()
        for k in (2, 1, 3):
            self.start(2 + k, self.line(), self.device(not self.x_first, k))
        self.start(6, self.line(), self.sibling())

    def third(self):
        for k in (1, 3, 2):
            self.copy(2 + k, self.line(k), self.device(not self.x_first, k)).wait_recv()
            self.start(6 + k, self.line(k), self.sibling())

    def finish(self):
        for k in (0, 1, 3, 2):
            self.copy(6 + k, self.line(k, True), self.sibling()).wait_recv()
        for k in (1, 2, 3):
            self.copy(k - 1, self.slot(), self.device(self.x_first, k)).wait_send()
            self.copy(2 + k, self.line(), self.device(not self.x_first, k)).wait_send()
        for k in range(4):
            self.copy(6 + k, self.line(k), self.sibling()).wait_send()


class EagerFlow(Flow):
    def at(self, b, k=0):
        _, xi, yi, core = self.place
        if self.x_first:
            return self.buf.at[(xi + 4 - b) % 4, (yi + 4 - k) % 4, core]
        return self.buf.at[(xi + 4 - k) % 4, (yi + 4 - b) % 4, core]

    def first(self):
        for k in (2, 1, 3):
            self.start(k - 1, self.at(0), self.device(self.x_first, k))
        for k in (2, 1, 3):
            self.start(2 + k, self.at(0), self.device(not self.x_first, k))

    def second(self):
        for b in (1, 3, 2):
            self.copy(b - 1, self.at(b), self.device(self.x_first, b)).wait_recv()
            for k in (2, 1, 3):
                self.start(2 + 3 * b + k, self.at(b), self.device(not self.x_first, k))
        self.start(15, self.line(), self.sibling())

    def third(self):
        for k in (1, 3, 2):
            for b in range(4):
                self.copy(2 + 3 * b + k, self.at(b, k), self.device(not self.x_first, k)).wait_recv()
            self.start(15 + k, self.line(k), self.sibling())

    def finish(self):
        for k in (0, 1, 3, 2):
            self.copy(15 + k, self.line(k, True), self.sibling()).wait_recv()
        for k in (1, 2, 3):
            self.copy(k - 1, self.at(0), self.device(self.x_first, k)).wait_send()
            for b in range(4):
                self.copy(2 + 3 * b + k, self.at(b), self.device(not self.x_first, k)).wait_send()
        for k in range(4):
            self.copy(15 + k, self.line(k), self.sibling()).wait_send()


def whole(ref):
    return ref[...].reshape(H, H)


def spread(inv_ref, child, s_ref, blocks_ref, zrow_ref, zt_ref):
    blocks_ref[:NB] = s_ref[...].reshape(NB, BLOCK, H)
    for p in range(NBF):
        zrow_ref[p] = blocks_ref[inv_ref[child, p]]
    zt_ref[:NB] = zrow_ref[...].reshape(FRONT, H).T.reshape(NB, BLOCK, FRONT)


def add_rows(inv_ref, child, zt_ref, ai_ref, a12_ref, low_ref, me):
    for p in range(NB):
        rows = pl.ds(p * BLOCK, BLOCK)
        block = zt_ref[inv_ref[child, p]]
        ai_ref[rows, :] = ai_ref[rows, :] + block[:, :H]
        a12_ref[rows, :] = a12_ref[rows, :] + block[:, H:]
    low_ref[...] = low_ref[...] + zt_ref[inv_ref[child, NB + me]]


def main_kernel(inv_ref, map_ref, leaf_ref, upper_ref, cov_ref, out_ref, *scratch):
    scratch = list(scratch)

    def take(n):
        got = scratch[:n]
        del scratch[:n]
        return got

    g11, g12, s_own, s_par = take(4), take(4), take(3), take(3)
    (gcov,) = take(1)
    ai, a12, gts, xts = take(4), take(4), take(4), take(4)
    blocks, zrow, zt, low, zt_up, rt, yt_ref, diag, col, row, sends, recvs, eager_sends, eager_recvs, z_sems = scratch
    blocks[NB] = jnp.zeros((BLOCK, H), F32)
    zt[NB] = jnp.zeros((BLOCK, FRONT), F32)
    for xt_ref in xts:
        xt_ref[NB] = jnp.zeros((BLOCK, 2 * BLOCK), F32)

    leaf = lax.axis_index("leaf")
    me = lax.axis_index("front")
    xi, yi, core = me // 8, (me // 2) % 4, me % 2
    place = (leaf, xi, yi, core)
    across_to = [(leaf + d - 2 * d * ((leaf // d) % 2), me) for d in (1, 2, 4)]
    partners = [(leaf, ((xi + k) % 4) * 8 + yi * 2 + core) for k in (1, 2, 3)]
    partners += [(leaf, xi * 8 + ((yi + k) % 4) * 2 + core) for k in (1, 2, 3)]
    partners += [(leaf, me + 1 - 2 * core)] + across_to
    barrier = pltpu.get_barrier_semaphore()
    for device in partners:
        pl.semaphore_signal(barrier, inc=1, device_id=device, device_id_type=MESH)

    def eager(buf, x_first, number):
        return EagerFlow(buf, x_first, number, place, eager_sends, eager_recvs)

    def lazy(buf, x_first, number):
        return Flow(buf, x_first, number, place, sends, recvs)

    front_flows = [(eager(g11[0], True, 0), eager(g12[0], False, 1))]
    front_flows += [
        (lazy(g11[h], True, 2 * h - 2), lazy(g12[h], False, 2 * h - 1)) for h in range(1, LEVELS)
    ]
    cov_flow = lazy(gcov, True, 6)
    schur_flows = [
        (eager(s_own[h], True, 2 * h + 2), eager(s_par[h], False, 2 * h + 3)) for h in range(LEVELS - 1)
    ]
    own_child = [leaf, 8 + leaf // 2, 12 + leaf // 4]
    par_child = [
        base + n + 1 - 2 * (n % 2) for base, n in ((0, leaf), (8, leaf // 2), (12, leaf // 4))
    ]
    nodes = [None, leaf // 2, 4 + leaf // 4, 6]

    def open_flows(height):
        front_flows[height][0].put(upper_ref[nodes[height], 0, :, :H])
        front_flows[height][1].put(upper_ref[nodes[height], 0, :, H:])
        for flow in front_flows[height]:
            flow.first()

    def pumps(flows, opening):
        def second():
            for flow in flows:
                flow.second()

        def third():
            for flow in flows:
                flow.third()

        def finish():
            for flow in flows:
                flow.finish()

        return (opening, second, third, finish)

    front_flows[0][0].put(leaf_ref[0, 0, :, :H])
    front_flows[0][1].put(leaf_ref[0, 0, :, H:])
    pl.semaphore_wait(barrier, len(partners))
    for flow in front_flows[0]:
        flow.first()
    for flow in front_flows[0]:
        flow.second()
    front_flows[0][0].third()
    front_flows[0][0].finish()
    ai[0][...] = whole(g11[0])
    low[...] = leaf_ref[0, 1]

    for height in range(LEVELS):
        last = height == LEVELS - 1
        if height > 0:
            ai[height][...] = whole(g11[height])
            a12[height][...] = whole(g12[height])
            low[...] = upper_ref[nodes[height], 1]
            link = height - 1
            own_flow, par_flow = schur_flows[link]
            own_flow.finish()
            spread(inv_ref, own_child[link], s_own[link], blocks, zrow, zt)
            par_flow.third()
            add_rows(inv_ref, own_child[link], zt, ai[height], a12[height], low, me)
            par_flow.finish()
            spread(inv_ref, par_child[link], s_par[link], blocks, zrow, zt)
            add_rows(inv_ref, par_child[link], zt, ai[height], a12[height], low, me)
        if last:
            def opening():
                cov_flow.put(cov_ref[...])
                cov_flow.first()

            invert_in_place(ai[height], diag, col, row, pumps([cov_flow], opening))
        else:
            def opening(above=height + 1):
                if above == 1:
                    front_flows[0][1].third()
                open_flows(above)

            invert_in_place(ai[height], diag, col, row, pumps(front_flows[height + 1], opening))
            if height == 0:
                front_flows[0][1].finish()
                a12[0][...] = whole(g12[0])
            own_flow, par_flow = schur_flows[height]
            g = dot(low[:, :H], ai[height][...])
            own_flow.put(low[:, H:] - dot(g, a12[height][...]))
            across = pltpu.make_async_remote_copy(
                src_ref=s_own[height].at[xi, yi, core], dst_ref=s_par[height].at[xi, yi, core],
                send_sem=z_sems.at[height, 0], recv_sem=z_sems.at[height, 1],
                device_id=across_to[height], device_id_type=MESH,
            )
            across.start()
            own_flow.first()
        if height == 0:
            rows = lax.broadcasted_iota(jnp.int32, (H, 2 * BLOCK), 0)
            cols = lax.broadcasted_iota(jnp.int32, (H, 2 * BLOCK), 1)
            za = ((rows == me * BLOCK + cols) & (cols < BLOCK)).astype(F32)
            zb = ((rows == (me - 1) * BLOCK + cols) & (cols >= BLOCK)).astype(F32)
        else:
            for p in range(NBF):
                zt_up[pl.ds(p * BLOCK, BLOCK), :] = xts[height - 1][inv_ref[own_child[height - 1], p]]
            za, zb = zt_up[:H, :], zt_up[H:, :]
        gt = dot(ai[height][...], za)
        gts[height][...] = gt
        xt = zb - dot_tn(a12[height][...], gt)
        xts[height][:NB] = xt.reshape(NB, BLOCK, 2 * BLOCK)
        if not last:
            across.wait_recv()
            par_flow.first()
            own_flow.second()
            par_flow.second()
            own_flow.third()
            across.wait_send()

    yt_ref[...] = dot(whole(gcov), xt)
    for height in range(LEVELS - 1, -1, -1):
        yt = yt_ref[...]
        top = gts[height][...] - dot(ai[height][...], dot(a12[height][...], yt))
        rt[:NB] = top.reshape(NB, BLOCK, 2 * BLOCK)
        rt[NB:] = yt.reshape(NB, BLOCK, 2 * BLOCK)
        if height > 0:
            for a in range(NB):
                yt_ref[pl.ds(a * BLOCK, BLOCK), :] = rt[map_ref[own_child[height - 1], a]]
    out_ref[...] = rt[...].reshape(FRONT, 2 * BLOCK).T.reshape(1, 2, BLOCK, FRONT)


def body(fronts_leaf, fronts_upper, block_map, parent_cov):
    hit = block_map[:, None, :] == jnp.arange(NBF, dtype=jnp.int32)[None, :, None]
    where_from = jnp.arange(NB, dtype=jnp.int32) - NB
    inverse_maps = NB + jnp.sum(jnp.where(hit, where_from, 0), -1, dtype=jnp.int32)
    vm = pl.BlockSpec(memory_space=pltpu.VMEM)
    sm = pl.BlockSpec(memory_space=pltpu.SMEM)
    plane = pltpu.VMEM((4, 4, 2, BLOCK, H), F32)
    square = pltpu.VMEM((H, H), F32)
    thin = pltpu.VMEM((H, 2 * BLOCK), F32)
    parts = pltpu.VMEM((NB + 1, BLOCK, 2 * BLOCK), F32)
    sems = pltpu.SemaphoreType.DMA
    return pl.pallas_call(
        main_kernel,
        out_shape=jax.ShapeDtypeStruct((1, 2, BLOCK, FRONT), F32),
        in_specs=[sm, sm, vm, vm, vm],
        out_specs=vm,
        scratch_shapes=[plane] * 15 + [square] * 8 + [thin] * 4 + [parts] * 4
        + [
            pltpu.VMEM((NB + 1, BLOCK, H), F32),
            pltpu.VMEM((NBF, BLOCK, H), F32),
            pltpu.VMEM((NB + 1, BLOCK, FRONT), F32),
            pltpu.VMEM((BLOCK, FRONT), F32),
            pltpu.VMEM((FRONT, 2 * BLOCK), F32),
            pltpu.VMEM((NBF, BLOCK, 2 * BLOCK), F32),
            pltpu.VMEM((H, 2 * BLOCK), F32),
            pltpu.VMEM((128, 128), F32),
            pltpu.VMEM((H, 128), F32),
            pltpu.VMEM((128, H), F32),
            sems((7, 10)), sems((7, 10)), sems((8, 19)), sems((8, 19)), sems((3, 2)),
        ],
        compiler_params=pltpu.CompilerParams(
            collective_id=0, has_side_effects=True, vmem_limit_bytes=56 * 2**20
        ),
    )(inverse_maps, block_map, fronts_leaf, fronts_upper, parent_cov)


def solution(mesh):
    placed = (P("leaf", None, "front", None), P(None, None, "front", None), P(), P("front", None))
    return jax.shard_map(
        body, mesh=mesh, in_specs=placed, out_specs=P("leaf", None, "front", None), check_vma=False
    )
```
